32 devices in a mesh: groups: 2 (over x), tok: 16 (over z, y, core).
Axes of the slice: x: 2, y: 2, z: 4, core: 2. Of those that a mesh axis runs over, the one named last changes fastest.
Arguments:
- queries: bfloat16 [384, 32, 4096], P('tok', 'groups'), parts along dimension 1, may hold values from -32 to 32
- cross_query_rows: bfloat16 [384, 32, 4096], P('tok', 'groups'), parts along dimension 1, may hold values from -32 to 32
- prompt_key_rows: bfloat16 [384, 32, 512], P('tok', 'groups'), parts along dimension 1, may hold values from -32 to 32
- prompt_value_rows: bfloat16 [384, 32, 512], P('tok', 'groups'), parts along dimension 1, may hold values from -6 to 6
- image_cache: bfloat16 [2, 4, 512, 512], P(None, 'groups'), parts along dimension 1, may hold values from -32 to 32
- query_head_gate: float32 [32], replicated, may hold values from -2 to 2
- lengths: int32 [32], P('groups'), parts along dimension 0, may hold values from 1 to 384, 3072 in all
- owner_slot: int32 [32], P('groups'), parts along dimension 0, may hold values from 0 to 15, each once
- image_index: int32 [32], P('groups'), parts along dimension 0, may hold values from 0 to 1
Outputs:
- attended: bfloat16 [384, 32, 4096], P('tok', 'groups'), parts along dimension 1
- kv_cache: bfloat16 [2, 32, 384, 512], P(None, ('groups', 'tok')), parts along dimension 1
The draws below stay inside these ranges and needn't reach their ends.
There are 2 independent parts, one for each index of `groups`. The reference program is written for one: setup_inputs(seed, part) draws one part's arguments, and reference() takes and returns one part's arrays. A program takes and returns all parts, laid end to end along the dimension named above; an argument that names none is the same for every part. Nothing has to cross between parts.
Inputs may be any that keep to these rules, and one draw needn't show every extreme that they name: `lengths`: some request has length 384. `owner_slot`: each slot owns exactly one request.
All inputs are finite; a program needn't handle non-finite values.
Results may differ from the reference program's by a relative error of at most 0.005.
Values may be sent and summed in bfloat16 or wider, within the bound.
A program may use at most 128 MiB of HBM per device.

```python
import math
import jax
import jax.numpy as jnp
import numpy as np
from jax import lax

HQ = 32
KEY_HEAD_COUNT = 4
HEAD_WIDTH = 128
QUERY_PER_KEY = 8
SLOT_LENGTH = 384
IMAGE_ROW_COUNT = 512
IMAGE_COUNT = 2
REQUEST_COUNT = 16


def row_scales(key, shape, lower, upper):
    return jnp.exp(jax.random.uniform(key, shape, jnp.float32, jnp.log(lower), jnp.log(upper)))


def draw_queries(key, part):
    key = jax.random.fold_in(key, 1)
    return jnp.clip(jax.random.normal(key, (SLOT_LENGTH, REQUEST_COUNT, HQ * HEAD_WIDTH), jnp.float32), -4.0, 4.0).astype(jnp.bfloat16)


def draw_cross_query_rows(key, part):
    key = jax.random.fold_in(key, 4)
    return jnp.clip(jax.random.normal(key, (SLOT_LENGTH, REQUEST_COUNT, HQ * HEAD_WIDTH), jnp.float32), -4.0, 4.0).astype(jnp.bfloat16)


def draw_prompt_key_rows(key, part):
    key = jax.random.fold_in(key, 2)
    scale_key = jax.random.fold_in(key, 20)
    base_offset = jnp.clip(jax.random.normal(key, (SLOT_LENGTH, REQUEST_COUNT, KEY_HEAD_COUNT * HEAD_WIDTH), jnp.float32), -4.0, 4.0)
    return (base_offset * row_scales(scale_key, (SLOT_LENGTH, REQUEST_COUNT, 1), 0.5, 2.0)).astype(jnp.bfloat16)


def draw_image_cache(key, part):
    key = jax.random.fold_in(key, 3)
    key_portion = jax.random.fold_in(key, 30)
    value_portion = jax.random.fold_in(key, 31)
    scale_key = jax.random.fold_in(key, 32)
    image_key_rows = jnp.clip(jax.random.normal(key_portion, (IMAGE_COUNT, IMAGE_ROW_COUNT, KEY_HEAD_COUNT * HEAD_WIDTH), jnp.float32), -4.0, 4.0)
    image_key_rows = image_key_rows * row_scales(scale_key, (IMAGE_COUNT, IMAGE_ROW_COUNT, 1), 0.5, 2.0)
    image_value_rows = jnp.clip(jax.random.normal(value_portion, (IMAGE_COUNT, IMAGE_ROW_COUNT, KEY_HEAD_COUNT * HEAD_WIDTH), jnp.float32), -4.0, 4.0)
    return jnp.stack([image_key_rows, image_value_rows]).astype(jnp.bfloat16)


def with_ends(array, rng, smallest, high):
    extent = array.shape
    place = [jax.random.randint(jax.random.fold_in(rng, axis), (), 0, extent[axis]) for axis in range(len(extent))]
    array = array.at[tuple(place)].set(smallest)
    longest = extent.index(max(extent))
    place[longest] = (place[longest] + 1) % extent[longest]
    return array.at[tuple(place)].set(high)


def levels(stream_key, shape, shards, least, high):
    gain, own = 1.0, jax.random.fold_in(stream_key, 6)
    for dim, shards_of in shards:
        steps = jnp.exp(jax.random.uniform(jax.random.fold_in(own, dim), (shards_of,), jnp.float32, least / len(shards), high / len(shards)))
        gain = gain * jnp.repeat(steps, shape[dim] // shards_of).reshape([-1 if axis == dim else 1 for axis in range(len(shape))])
    return gain


def split_up(amount, total, bound, lean):
    weights = [(1 << 20) // math.isqrt(rank ** lean) + 1 for rank in range(2, amount + 1)]
    surplus, counts = total - bound - (amount - 1), [1] * (amount - 1)
    while surplus > 0:
        candidates = [i for i in range(amount - 1) if counts[i] < bound]
        pool, left = sum([weights[i] for i in candidates]), surplus
        for i in candidates:
            more = min(bound - counts[i], max(1, left * weights[i] // pool), surplus)
            counts[i] = counts[i] + more
            surplus = surplus - more
    return np.array([bound] + counts)


def uneven_parts(key, number_of, total, most, skew):
    if number_of == 2:
        one = jax.random.randint(key, (), max(1, total - most), min(most, total - 1) + 1)
        return jnp.stack([one, total - one])
    sizes = jnp.asarray(split_up(number_of, total, most, skew), jnp.int32)
    couples = (number_of - 1) // 2
    giver, taker = sizes[1:1 + 2 * couples:2], sizes[2:2 + 2 * couples:2]
    margin = jnp.minimum(giver - 1, most - taker)
    shifted = jax.random.randint(jax.random.fold_in(key, 1), (couples,), 0, 1 << 20) % (margin + 1)
    sizes = sizes.at[1:1 + 2 * couples:2].set(giver - shifted).at[2:2 + 2 * couples:2].set(taker + shifted)
    return sizes[jax.random.permutation(jax.random.fold_in(key, 2), number_of)]


def scatter_about(rng, shape, scale, bound, cuts=(), kind=jnp.bfloat16):
    entries = jax.random.normal(rng, shape, jnp.float32) * scale
    if len(cuts) > 0:
        entries = levels(rng, shape, cuts, -0.22, 0.18) * entries
    return jnp.clip(entries, min=-bound, max=bound).astype(kind)


def setup_inputs(seed: int = 0, part: int = 0) -> dict:
    splits = jax.random.split(jax.random.key(seed), 10)
    part_splits = jax.random.split(jax.random.fold_in(splits[9], part), 10)
    return {
        "queries": draw_queries(jax.random.fold_in(jax.random.fold_in(splits[9], part), 71), part),
        "cross_query_rows": draw_cross_query_rows(jax.random.fold_in(jax.random.fold_in(splits[9], part), 71), part),
        "prompt_key_rows": draw_prompt_key_rows(jax.random.fold_in(jax.random.fold_in(splits[9], part), 71), part),
        "prompt_value_rows": scatter_about(part_splits[3], (SLOT_LENGTH, REQUEST_COUNT, KEY_HEAD_COUNT * HEAD_WIDTH), 1.0, 6.0, ((0, 16),)),
        "image_cache": draw_image_cache(jax.random.fold_in(jax.random.fold_in(splits[9], part), 71), part),
        "query_head_gate": jnp.clip(jax.random.uniform(splits[5], (HQ,), jnp.float32, -2.0, 2.0), -2.0, 2.0),
        "lengths": uneven_parts(part_splits[6], REQUEST_COUNT, REQUEST_COUNT * SLOT_LENGTH // 2, SLOT_LENGTH, 2).astype(jnp.int32),
        "owner_slot": jax.random.permutation(part_splits[7], REQUEST_COUNT).astype(jnp.int32),
        "image_index": with_ends(jax.random.randint(part_splits[8], (REQUEST_COUNT,), 0, IMAGE_COUNT), jax.random.fold_in(part_splits[8], 1), 0, IMAGE_COUNT - 1).astype(jnp.int32),
    }


def attend_rows(query_head_rows, key_head_rows, value_head_rows, allowed):
    scores = jnp.einsum('lgqd,mgd->lgqm', query_head_rows, key_head_rows) / math.sqrt(HEAD_WIDTH)
    if allowed is not None:
        scores = jnp.where(allowed[:, None, None, :], scores, -1e+30)
    row_top = lax.optimization_barrier(jnp.max(scores, axis=-1, keepdims=True))
    weights = jnp.exp(scores - row_top)
    row_total = lax.optimization_barrier(jnp.sum(weights, axis=-1, keepdims=True))
    rounded = lax.optimization_barrier(weights.astype(jnp.bfloat16)).astype(jnp.float32)
    return jnp.einsum('lgqm,mgd->lgqd', rounded, value_head_rows) / row_total

def reference(queries, cross_query_rows, prompt_key_rows, prompt_value_rows, image_cache, query_head_gate, lengths, owner_slot, image_index):
    positions = jnp.arange(SLOT_LENGTH, dtype=jnp.int32)
    squashed_gate = jnp.tanh(query_head_gate).reshape(KEY_HEAD_COUNT, QUERY_PER_KEY)

    def one_request(request_number):
        query_head_rows = lax.dynamic_index_in_dim(queries, request_number, 1, keepdims=False).astype(jnp.float32).reshape(SLOT_LENGTH, KEY_HEAD_COUNT, QUERY_PER_KEY, HEAD_WIDTH)
        cross_head_rows = lax.dynamic_index_in_dim(cross_query_rows, request_number, 1, keepdims=False).astype(jnp.float32).reshape(SLOT_LENGTH, KEY_HEAD_COUNT, QUERY_PER_KEY, HEAD_WIDTH)
        key_head_rows = lax.dynamic_index_in_dim(prompt_key_rows, request_number, 1, keepdims=False).astype(jnp.float32).reshape(SLOT_LENGTH, KEY_HEAD_COUNT, HEAD_WIDTH)
        value_head_rows = lax.dynamic_index_in_dim(prompt_value_rows, request_number, 1, keepdims=False).astype(jnp.float32).reshape(SLOT_LENGTH, KEY_HEAD_COUNT, HEAD_WIDTH)
        length = lax.dynamic_index_in_dim(lengths, request_number, 0, keepdims=False)
        picture = lax.dynamic_index_in_dim(image_index, request_number, 0, keepdims=False)
        image_row_block = lax.dynamic_index_in_dim(image_cache, picture, 1, keepdims=False).astype(jnp.float32)
        image_key_rows = image_row_block[0].reshape(IMAGE_ROW_COUNT, KEY_HEAD_COUNT, HEAD_WIDTH)
        image_value_rows = image_row_block[1].reshape(IMAGE_ROW_COUNT, KEY_HEAD_COUNT, HEAD_WIDTH)
        allowed = positions[None, :] <= positions[:, None]
        causal_out = attend_rows(query_head_rows, key_head_rows, value_head_rows, allowed)
        self_out = lax.optimization_barrier(causal_out.astype(jnp.bfloat16)).astype(jnp.float32)
        cross_out = attend_rows(cross_head_rows, image_key_rows, image_value_rows, None)
        combined = self_out + squashed_gate[None, :, :, None] * cross_out
        combined = jnp.where((positions < length)[:, None, None, None], combined, 0.0)
        return combined.reshape(SLOT_LENGTH, HQ * HEAD_WIDTH).astype(jnp.bfloat16)
    attended = lax.map(one_request, jnp.arange(REQUEST_COUNT, dtype=jnp.int32))
    attended = jnp.transpose(attended, (1, 0, 2))
    slot_request = jnp.argsort(owner_slot).astype(jnp.int32)
    live = positions[None, :] < lengths[slot_request][:, None]
    cache_keys = jnp.transpose(prompt_key_rows[:, slot_request], (1, 0, 2))
    cache_values = jnp.transpose(prompt_value_rows[:, slot_request], (1, 0, 2))
    cache_keys = jnp.where(live[:, :, None], cache_keys, jnp.zeros_like(cache_keys))
    cache_values = jnp.where(live[:, :, None], cache_values, jnp.zeros_like(cache_values))
    kv_cache = jnp.stack([cache_keys, cache_values])
    return (attended, kv_cache)
```

```python
import functools
import math

import jax
import jax.numpy as jnp
from jax import lax
from jax.experimental import pallas as pl
from jax.experimental.pallas import tpu as pltpu
from jax.sharding import PartitionSpec as P

HQ = 32
KEY_HEAD_COUNT = 4
HEAD_WIDTH = 128
QUERY_PER_KEY = 8
SCALE = 1.0 / math.sqrt(HEAD_WIDTH)
VMEM_LIMIT = 48 * 1024 * 1024

NT = (((1,), (1,)), ((), ()))


def attend(queries, keys, values, bias):
    scores = lax.dot_general(queries, keys, NT, preferred_element_type=jnp.float32) * SCALE
    if bias is not None:
        scores = scores + bias
    top = jnp.max(scores, axis=-1, keepdims=True)
    weights = jnp.exp(scores - top)
    total = jnp.sum(weights, axis=-1, keepdims=True)
    weighted = jnp.dot(weights.astype(jnp.bfloat16), values, preferred_element_type=jnp.float32)
    return weighted, total


def cross_kernel(local, lengths_ref, image_ref, first_ref, query_ref, cache_ref, gate_ref, out_ref):
    request = pl.program_id(0)
    live = lengths_ref[request] > first_ref[0]

    @pl.when(live)
    def _():
        picture = image_ref[request]
        for group in range(KEY_HEAD_COUNT):
            lanes = slice(group * HEAD_WIDTH, (group + 1) * HEAD_WIDTH)
            weighted, total = attend(
                query_ref[0, group], cache_ref[0, picture, :, lanes], cache_ref[1, picture, :, lanes], None
            )
            out_ref[0, group] = (weighted * (gate_ref[group] / total)).astype(out_ref.dtype)

    @pl.when(jnp.logical_not(live))
    def _():
        out_ref[...] = jnp.zeros_like(out_ref)


def causal_kernel(local, slot, lengths_ref, first_ref, query_ref, kv_ref, cross_ref, out_ref):
    request = pl.program_id(0)
    first = first_ref[0]
    length = lengths_ref[request]
    live = length > first
    rows = QUERY_PER_KEY * local
    needed = first + local

    def run(keys):
        row = lax.broadcasted_iota(jnp.int32, (rows, keys), 0)
        position = first + lax.rem(row, local)
        key = lax.broadcasted_iota(jnp.int32, (rows, keys), 1)
        bias = jnp.where(key <= position, 0.0, -1e30)
        alive = position[:, :HEAD_WIDTH] < length
        for group in range(KEY_HEAD_COUNT):
            lanes = slice(group * HEAD_WIDTH, (group + 1) * HEAD_WIDTH)
            value_lanes = slice((KEY_HEAD_COUNT + group) * HEAD_WIDTH, (KEY_HEAD_COUNT + group + 1) * HEAD_WIDTH)
            weighted, total = attend(
                query_ref[0, group], kv_ref[0, :keys, lanes], kv_ref[0, :keys, value_lanes], bias
            )
            own = (weighted / total).astype(jnp.bfloat16).astype(jnp.float32)
            combined = own + cross_ref[0, group].astype(jnp.float32)
            out_ref[0, group] = jnp.where(alive, combined, 0.0).astype(out_ref.dtype)

    for keys in range(128, slot + 1, 128):
        @pl.when(live & (needed <= keys) & (needed > keys - 128))
        def _():
            run(keys)

    @pl.when(jnp.logical_not(live))
    def _():
        out_ref[...] = jnp.zeros_like(out_ref)


def shards(
    queries,
    cross_query_rows,
    prompt_key_rows,
    prompt_value_rows,
    image_cache,
    query_head_gate,
    lengths,
    owner_slot,
    image_index,
):
    local, requests, _ = queries.shape
    devices = lax.axis_size("tok")
    slot = local * devices
    rank = lax.axis_index("tok")
    rows = QUERY_PER_KEY * local
    first = jnp.full((1,), rank * local, jnp.int32)

    kv = jnp.concatenate([prompt_key_rows, prompt_value_rows], axis=-1)
    gathered = lax.all_gather(kv, "tok", axis=0, tiled=True)
    by_request = jnp.transpose(gathered, (1, 0, 2))

    def by_head(array):
        array = array.reshape(local, requests, KEY_HEAD_COUNT, QUERY_PER_KEY, HEAD_WIDTH)
        return jnp.transpose(array, (1, 2, 3, 0, 4)).reshape(requests, KEY_HEAD_COUNT, rows, HEAD_WIDTH)

    gate = jnp.tanh(query_head_gate).reshape(KEY_HEAD_COUNT, QUERY_PER_KEY, 1)
    gate = jnp.broadcast_to(gate, (KEY_HEAD_COUNT, QUERY_PER_KEY, local)).reshape(KEY_HEAD_COUNT, rows, 1)

    head_block = pl.BlockSpec((1, KEY_HEAD_COUNT, rows, HEAD_WIDTH), lambda r, *_: (r, 0, 0, 0))
    head_shape = jax.ShapeDtypeStruct((requests, KEY_HEAD_COUNT, rows, HEAD_WIDTH), jnp.bfloat16)
    params = pltpu.CompilerParams(vmem_limit_bytes=VMEM_LIMIT)
    flops = requests * HQ * local * HEAD_WIDTH * 4
    cross = pl.pallas_call(
        functools.partial(cross_kernel, local),
        grid_spec=pltpu.PrefetchScalarGridSpec(
            num_scalar_prefetch=3,
            grid=(requests,),
            in_specs=[
                head_block,
                pl.BlockSpec(image_cache.shape, lambda r, *_: (0, 0, 0, 0)),
                pl.BlockSpec(gate.shape, lambda r, *_: (0, 0, 0)),
            ],
            out_specs=head_block,
        ),
        out_shape=head_shape,
        compiler_params=params,
        cost_estimate=pl.CostEstimate(flops=flops * 512, bytes_accessed=8 << 20, transcendentals=0),
        name="cross",
    )(lengths, image_index, first, by_head(cross_query_rows), image_cache, gate)

    attended = pl.pallas_call(
        functools.partial(causal_kernel, local, slot),
        grid_spec=pltpu.PrefetchScalarGridSpec(
            num_scalar_prefetch=2,
            grid=(requests,),
            in_specs=[
                head_block,
                pl.BlockSpec((1, slot, 2 * KEY_HEAD_COUNT * HEAD_WIDTH), lambda r, *_: (r, 0, 0)),
                head_block,
            ],
            out_specs=head_block,
        ),
        out_shape=head_shape,
        compiler_params=params,
        cost_estimate=pl.CostEstimate(flops=flops * slot, bytes_accessed=24 << 20, transcendentals=0),
        name="causal",
    )(lengths, first, by_head(queries), by_request, cross)
    attended = attended.reshape(requests, KEY_HEAD_COUNT, QUERY_PER_KEY, local, HEAD_WIDTH)
    attended = jnp.transpose(attended, (3, 0, 1, 2, 4)).reshape(local, requests, HQ * HEAD_WIDTH)

    own_request = jnp.argmax(owner_slot == rank).astype(jnp.int32)
    length = lax.dynamic_index_in_dim(lengths, own_request, 0, keepdims=False)
    own = lax.dynamic_index_in_dim(by_request, own_request, 0, keepdims=False)
    own = jnp.where(jnp.arange(slot, dtype=jnp.int32)[:, None] < length, own, jnp.zeros((), own.dtype))
    width = KEY_HEAD_COUNT * HEAD_WIDTH
    kv_cache = jnp.stack([own[:, :width], own[:, width:]])[:, None]
    return attended, kv_cache


def solution(mesh):
    placed = (
        P("tok", "groups", None),
        P("tok", "groups", None),
        P("tok", "groups", None),
        P("tok", "groups", None),
        P(None, "groups", None, None),
        P(),
        P("groups"),
        P("groups"),
        P("groups"),
    )
    return jax.shard_map(
        shards,
        mesh=mesh,
        in_specs=placed,
        out_specs=(P("tok", "groups", None), P(None, ("groups", "tok"), None, None)),
        check_vma=False,
    )
```

```python
import functools
import math

import jax
import jax.numpy as jnp
from jax import lax
from jax.experimental import pallas as pl
from jax.experimental.pallas import tpu as pltpu
from jax.sharding import PartitionSpec as P

HQ = 32
KEY_HEAD_COUNT = 4
HEAD_WIDTH = 128
QUERY_PER_KEY = 8
SCALE = 1.0 / math.sqrt(HEAD_WIDTH)
VMEM_LIMIT = 48 * 1024 * 1024

NT = (((1,), (1,)), ((), ()))


def attend(queries, keys, values, bias):
    scores = lax.dot_general(queries, keys, NT, preferred_element_type=jnp.float32) * SCALE
    if bias is not None:
        scores = scores + bias
    top = jnp.max(scores, axis=-1, keepdims=True)
    weights = jnp.exp(scores - top)
    total = jnp.sum(weights, axis=-1, keepdims=True)
    weighted = jnp.dot(weights.astype(jnp.bfloat16), values, preferred_element_type=jnp.float32)
    return weighted, total


def cross_kernel(local, lengths_ref, image_ref, first_ref, query_ref, cache_ref, gate_ref, out_ref):
    request = pl.program_id(0)
    live = lengths_ref[request] > first_ref[0]

    @pl.when(live)
    def _():
        picture = image_ref[request]
        for group in range(KEY_HEAD_COUNT):
            lanes = slice(group * HEAD_WIDTH, (group + 1) * HEAD_WIDTH)
            weighted, total = attend(
                query_ref[0, group], cache_ref[0, picture, :, lanes], cache_ref[1, picture, :, lanes], None
            )
            out_ref[0, group] = (weighted * (gate_ref[group] / total)).astype(out_ref.dtype)

    @pl.when(jnp.logical_not(live))
    def _():
        out_ref[...] = jnp.zeros_like(out_ref)


def causal_kernel(local, slot, lengths_ref, first_ref, query_ref, kv_ref, cross_ref, out_ref):
    request = pl.program_id(0)
    first = first_ref[0]
    length = lengths_ref[request]
    live = length > first
    rows = QUERY_PER_KEY * local
    needed = first + local

    def run(keys):
        row = lax.broadcasted_iota(jnp.int32, (rows, keys), 0)
        position = first + lax.rem(row, local)
        key = lax.broadcasted_iota(jnp.int32, (rows, keys), 1)
        bias = jnp.where(key <= position, 0.0, -1e30)
        alive = position[:, :HEAD_WIDTH] < length
        for group in range(KEY_HEAD_COUNT):
            lanes = slice(group * HEAD_WIDTH, (group + 1) * HEAD_WIDTH)
            value_lanes = slice((KEY_HEAD_COUNT + group) * HEAD_WIDTH, (KEY_HEAD_COUNT + group + 1) * HEAD_WIDTH)
            weighted, total = attend(
                query_ref[0, group], kv_ref[0, :keys, lanes], kv_ref[0, :keys, value_lanes], bias
            )
            own = (weighted / total).astype(jnp.bfloat16).astype(jnp.float32)
            combined = own + cross_ref[0, group].astype(jnp.float32)
            out_ref[0, group] = jnp.where(alive, combined, 0.0).astype(out_ref.dtype)

    for keys in range(128, slot + 1, 128):
        @pl.when(live & (needed <= keys) & (needed > keys - 128))
        def _():
            run(keys)

    @pl.when(jnp.logical_not(live))
    def _():
        out_ref[...] = jnp.zeros_like(out_ref)


def shards(
    queries,
    cross_query_rows,
    prompt_key_rows,
    prompt_value_rows,
    image_cache,
    query_head_gate,
    lengths,
    owner_slot,
    image_index,
):
    local, requests, _ = queries.shape
    devices = lax.axis_size("tok")
    slot = local * devices
    rank = lax.axis_index("tok")
    rows = QUERY_PER_KEY * local
    first = jnp.full((1,), rank * local, jnp.int32)

    kv = jnp.concatenate([prompt_key_rows, prompt_value_rows], axis=-1)
    gathered = lax.all_gather(kv, "tok", axis=0, tiled=True)
    by_request = jnp.transpose(gathered, (1, 0, 2))

    def by_head(array):
        array = array.reshape(local, requests, KEY_HEAD_COUNT, QUERY_PER_KEY, HEAD_WIDTH)
        return jnp.transpose(array, (1, 2, 3, 0, 4)).reshape(requests, KEY_HEAD_COUNT, rows, HEAD_WIDTH)

    gate = jnp.tanh(query_head_gate).reshape(KEY_HEAD_COUNT, QUERY_PER_KEY, 1)
    gate = jnp.broadcast_to(gate, (KEY_HEAD_COUNT, QUERY_PER_KEY, local)).reshape(KEY_HEAD_COUNT, rows, 1)

    head_block = pl.BlockSpec((1, KEY_HEAD_COUNT, rows, HEAD_WIDTH), lambda r, *_: (r, 0, 0, 0))
    head_shape = jax.ShapeDtypeStruct((requests, KEY_HEAD_COUNT, rows, HEAD_WIDTH), jnp.bfloat16)
    params = pltpu.CompilerParams(vmem_limit_bytes=VMEM_LIMIT)
    flops = requests * HQ * local * HEAD_WIDTH * 4
    cross = pl.pallas_call(
        functools.partial(cross_kernel, local),
        grid_spec=pltpu.PrefetchScalarGridSpec(
            num_scalar_prefetch=3,
            grid=(requests,),
            in_specs=[
                head_block,
                pl.BlockSpec(image_cache.shape, lambda r, *_: (0, 0, 0, 0)),
                pl.BlockSpec(gate.shape, lambda r, *_: (0, 0, 0)),
            ],
            out_specs=head_block,
        ),
        out_shape=head_shape,
        compiler_params=params,
        cost_estimate=pl.CostEstimate(flops=flops * 512, bytes_accessed=8 << 20, transcendentals=0),
        name="cross",
    )(lengths, image_index, first, by_head(cross_query_rows), image_cache, gate)

    attended = pl.pallas_call(
        functools.partial(causal_kernel, local, slot),
        grid_spec=pltpu.PrefetchScalarGridSpec(
            num_scalar_prefetch=2,
            grid=(requests,),
            in_specs=[
                head_block,
                pl.BlockSpec((1, slot, 2 * KEY_HEAD_COUNT * HEAD_WIDTH), lambda r, *_: (r, 0, 0)),
                head_block,
            ],
            out_specs=head_block,
        ),
        out_shape=head_shape,
        compiler_params=params,
        cost_estimate=pl.CostEstimate(flops=flops * slot, bytes_accessed=24 << 20, transcendentals=0),
        name="causal",
    )(lengths, first, by_head(queries), by_request, cross)
    attended = attended.reshape(requests, KEY_HEAD_COUNT, QUERY_PER_KEY, local, HEAD_WIDTH)
    attended = jnp.transpose(attended, (3, 0, 1, 2, 4)).reshape(local, requests, HQ * HEAD_WIDTH)

    own_request = jnp.argmax(owner_slot == rank).astype(jnp.int32)
    length = lax.dynamic_index_in_dim(lengths, own_request, 0, keepdims=False)
    own = lax.dynamic_index_in_dim(by_request, own_request, 0, keepdims=False)
    own = jnp.where(jnp.arange(slot, dtype=jnp.int32)[:, None] < length, own, jnp.zeros((), own.dtype))
    width = KEY_HEAD_COUNT * HEAD_WIDTH
    kv_cache = jnp.stack([own[:, :width], own[:, width:]])[:, None]
    return attended, kv_cache


CHUNK = 8


def rank_limit(requests, slot, first):
    if first == 0:
        return requests
    return min(requests, (requests * slot // 2 - requests) // first)


def relay_plan(chips, requests, slot, step_us):
    span = slot // chips
    limit = [rank_limit(requests, slot, span * chip) for chip in range(chips)]
    chunks = [(0, CHUNK), (CHUNK, requests)]

    def ranks(chip, chunk, up):
        lo, hi = chunks[chunk]
        top = limit[chip - chip % 2] if up else limit[chip]
        return lo, max(lo, min(hi, top))

    free = {}
    pending = [(0.0, chip, chip, "own", chunk) for chip in range(chips) for chunk in range(2)]
    events = [[] for _ in range(chips)]
    rate = span // 2 * 2048 / 45000.0
    while pending:
        pending.sort()
        time, chip, source, via, chunk = pending.pop(0)
        sends = []
        if via != "side":
            if chip + 2 < chips:
                sends.append((chip + 2, "up"))
            if source < (chip ^ 1):
                sends.append((chip ^ 1, "side"))
        kept = []
        for target, way in sends:
            lo, hi = ranks(target, chunk, way == "up")
            if hi > lo:
                start = max(time, free.get((chip, target), 0.0))
                end = start + rate * (hi - lo)
                free[chip, target] = end
                pending.append((end + 1.0, target, source, way, chunk))
                kept.append((target, lo, hi))
        got = ranks(chip, chunk, via == "up")
        need = ranks(chip, chunk, False)
        events[chip].append((int(time / step_us), source, via, chunk, got, need, kept))
    return events


def gather_kernel(
    devices, requests, local, plan, image_ref, picks_ref, query_ref, cache_ref, gate_ref,
    kv_ref, owned_ref, cross_ref, send_sem, recv_sem, pass_sem, owned_send, owned_recv, local_sem,
):
    me = lax.axis_index("tok")
    chip, core = lax.div(me, 2), lax.rem(me, 2)

    barrier = pltpu.get_barrier_semaphore()

    def greet(offset, carry):
        pl.semaphore_signal(
            barrier, inc=1, device_id={"tok": lax.rem(me + offset, devices)}, device_id_type=pl.DeviceIdType.MESH
        )
        return carry

    lax.fori_loop(1, devices, greet, 0)
    pl.semaphore_wait(barrier, devices - 1)

    keep = pltpu.make_async_copy(picks_ref.at[pl.ds(0, requests)], kv_ref.at[me], local_sem.at[0])
    keep_owned = pltpu.make_async_copy(picks_ref.at[requests + me], owned_ref.at[me], local_sem.at[1])
    keep.start()
    keep_owned.start()

    def block(source, lo, hi, own):
        if own:
            return picks_ref.at[pl.ds(lo, hi - lo)]
        return kv_ref.at[source, pl.ds(lo, hi - lo)]

    def relay(source, lo, hi, chunk, target, send, own):
        return pltpu.make_async_remote_copy(
            src_ref=block(source, lo, hi, own),
            dst_ref=kv_ref.at[source, pl.ds(lo, hi - lo)],
            send_sem=send,
            recv_sem=recv_sem.at[2 * source + chunk],
            device_id={"tok": target},
            device_id_type=pl.DeviceIdType.MESH,
        )

    def copies(number, position):
        _, source_chip, via, chunk, _, need, sends = plan[number][position]
        source = 2 * source_chip + core
        result = []
        for index, (target, lo, hi) in enumerate(sends):
            result.append(
                relay(source, lo, hi, chunk, 2 * target + core, send_sem.at[index, 2 * source_chip + chunk], via == "own")
            )
        if need[1] > need[0]:
            result.append(
                relay(source, need[0], need[1], chunk, 2 * number + 1 - core, pass_sem.at[2 * source_chip + chunk], via == "own")
            )
        return result

    def handle(number, position):
        _, source_chip, via, chunk, got, _, _ = plan[number][position]
        source = 2 * source_chip + core
        if via != "own":
            relay(source, got[0], got[1], chunk, me, pass_sem.at[0], False).wait_recv()
        for copy in copies(number, position):
            copy.start()

    def owned_copy(offset):
        target = lax.rem(me + offset, devices)
        return pltpu.make_async_remote_copy(
            src_ref=picks_ref.at[requests + target],
            dst_ref=owned_ref.at[me],
            send_sem=owned_send.at[offset],
            recv_sem=owned_recv.at[offset],
            device_id={"tok": target},
            device_id_type=pl.DeviceIdType.MESH,
        )

    def owned_start(offset, carry):
        owned_copy(offset).start()
        return carry

    def step(request, carry):
        for number in range(devices // 2):
            @pl.when(chip == number)
            def _():
                for when in sorted({event[0] for event in plan[number] if event[0] < requests}):
                    @pl.when(request == when)
                    def _():
                        for position, event in enumerate(plan[number]):
                            if event[0] == when:
                                handle(number, position)

        @pl.when(request == 0)
        def _():
            lax.fori_loop(1, devices, owned_start, 0)

        picture = image_ref[request]
        for group in range(KEY_HEAD_COUNT):
            lanes = slice(group * HEAD_WIDTH, (group + 1) * HEAD_WIDTH)
            weighted, total = attend(
                query_ref[request, group], cache_ref[0, picture, :, lanes], cache_ref[1, picture, :, lanes], None
            )
            cross_ref[request, group] = (weighted * (gate_ref[group] / total)).astype(cross_ref.dtype)
        return carry

    lax.fori_loop(0, requests, step, 0)

    for number in range(devices // 2):
        @pl.when(chip == number)
        def _():
            for position, event in enumerate(plan[number]):
                if event[0] >= requests:
                    handle(number, position)
            for position, event in enumerate(plan[number]):
                _, source_chip, _, chunk, _, need, _ = event
                if need[1] > need[0]:
                    relay(
                        2 * source_chip + 1 - core, need[0], need[1], chunk, me, pass_sem.at[0], False
                    ).wait_recv()
                for copy in copies(number, position):
                    copy.wait_send()

    def owned_wait(offset, carry):
        source = lax.rem(me + devices - offset, devices)
        pltpu.make_async_remote_copy(
            src_ref=picks_ref.at[requests + me],
            dst_ref=owned_ref.at[source],
            send_sem=owned_send.at[offset],
            recv_sem=owned_recv.at[offset],
            device_id={"tok": source},
            device_id_type=pl.DeviceIdType.MESH,
        ).wait_recv()
        owned_copy(offset).wait_send()
        return carry

    lax.fori_loop(1, devices, owned_wait, 0)
    keep.wait()
    keep_owned.wait()


def relayed_causal_kernel(local, slot, lengths_ref, rank_ref, first_ref, query_ref, kv_ref, cross_ref, out_ref):
    request = pl.program_id(0)
    first = first_ref[0]
    length = lengths_ref[request]
    live = length > first
    rows = QUERY_PER_KEY * local
    needed = first + local

    def run(keys):
        sources = -(-keys // local)
        row = lax.broadcasted_iota(jnp.int32, (rows, keys), 0)
        position = first + lax.rem(row, local)
        key = lax.broadcasted_iota(jnp.int32, (rows, keys), 1)
        allowed = key <= position
        alive = position[:, :HEAD_WIDTH] < length
        written = lax.broadcasted_iota(jnp.int32, (keys, HEAD_WIDTH), 0) < needed

        def rows_of(lane_block):
            lanes = slice(lane_block * HEAD_WIDTH, (lane_block + 1) * HEAD_WIDTH)
            pieces = kv_ref[:sources, 0, :, lanes].astype(jnp.float32)
            return pieces.reshape(sources * local, HEAD_WIDTH)[:keys]

        for group in range(KEY_HEAD_COUNT):
            key_rows = rows_of(group).astype(jnp.bfloat16)
            value_rows = jnp.where(written, rows_of(KEY_HEAD_COUNT + group), 0.0).astype(jnp.bfloat16)
            scores = lax.dot_general(query_ref[0, group], key_rows, NT, preferred_element_type=jnp.float32) * SCALE
            scores = jnp.where(allowed, scores, -1e30)
            top = jnp.max(scores, axis=-1, keepdims=True)
            weights = jnp.exp(scores - top)
            total = jnp.sum(weights, axis=-1, keepdims=True)
            weighted = jnp.dot(weights.astype(jnp.bfloat16), value_rows, preferred_element_type=jnp.float32)
            own = (weighted / total).astype(jnp.bfloat16).astype(jnp.float32)
            combined = own + cross_ref[0, group].astype(jnp.float32)
            out_ref[0, group] = jnp.where(alive, combined, 0.0).astype(out_ref.dtype)

    for keys in range(128, slot + 1, 128):
        @pl.when(live & (needed <= keys) & (needed > keys - 128))
        def _():
            run(keys)

    @pl.when(jnp.logical_not(live))
    def _():
        out_ref[...] = jnp.zeros_like(out_ref)


def relayed(
    queries,
    cross_query_rows,
    prompt_key_rows,
    prompt_value_rows,
    image_cache,
    query_head_gate,
    lengths,
    owner_slot,
    image_index,
):
    local, requests, _ = queries.shape
    devices = lax.axis_size("tok")
    slot = local * devices
    rank = lax.axis_index("tok")
    rows = QUERY_PER_KEY * local
    width = 2 * KEY_HEAD_COUNT * HEAD_WIDTH
    first = jnp.full((1,), rank * local, jnp.int32)
    ids = jnp.arange(requests, dtype=jnp.int32)

    longer = lengths[None, :] > lengths[:, None]
    tied = (lengths[None, :] == lengths[:, None]) & (ids[None, :] < ids[:, None])
    length_rank = jnp.sum((longer | tied).astype(jnp.int32), axis=1)
    chosen = jnp.concatenate([length_rank, owner_slot + requests]).reshape(2, requests)
    places = jnp.arange(2 * requests, dtype=jnp.int32)
    pick = (places[:, None, None] == chosen[None]).any(axis=1).astype(jnp.bfloat16)
    kv = jnp.concatenate([prompt_key_rows, prompt_value_rows], axis=-1)
    picks = jnp.einsum("sr,lrd->sld", pick, kv, preferred_element_type=jnp.float32).astype(jnp.bfloat16)

    def by_head(array):
        array = array.reshape(local, requests, KEY_HEAD_COUNT, QUERY_PER_KEY, HEAD_WIDTH)
        return jnp.transpose(array, (1, 2, 3, 0, 4)).reshape(requests, KEY_HEAD_COUNT, rows, HEAD_WIDTH)

    gate = jnp.tanh(query_head_gate).reshape(KEY_HEAD_COUNT, QUERY_PER_KEY, 1)
    gate = jnp.broadcast_to(gate, (KEY_HEAD_COUNT, QUERY_PER_KEY, local)).reshape(KEY_HEAD_COUNT, rows, 1)

    head_shape = jax.ShapeDtypeStruct((requests, KEY_HEAD_COUNT, rows, HEAD_WIDTH), jnp.bfloat16)
    anywhere = pl.BlockSpec(memory_space=pl.ANY)
    vmem = pl.BlockSpec(memory_space=pltpu.VMEM)
    plan = relay_plan(devices // 2, requests, slot, 1.5)
    kv_all, owned, cross = pl.pallas_call(
        functools.partial(gather_kernel, devices, requests, local, plan),
        in_specs=[pl.BlockSpec(memory_space=pltpu.SMEM), anywhere, vmem, vmem, vmem],
        out_specs=[anywhere, anywhere, vmem],
        out_shape=[
            jax.ShapeDtypeStruct((devices, requests, local, width), jnp.bfloat16),
            jax.ShapeDtypeStruct((devices, local, width), jnp.bfloat16),
            head_shape,
        ],
        scratch_shapes=[
            pltpu.SemaphoreType.DMA((2, devices)),
            pltpu.SemaphoreType.DMA((2 * devices,)),
            pltpu.SemaphoreType.DMA((devices,)),
            pltpu.SemaphoreType.DMA((devices,)),
            pltpu.SemaphoreType.DMA((devices,)),
            pltpu.SemaphoreType.DMA((2,)),
        ],
        compiler_params=pltpu.CompilerParams(
            collective_id=0, has_side_effects=True, vmem_limit_bytes=VMEM_LIMIT
        ),
        name="gather_cross",
    )(image_index, picks, by_head(cross_query_rows), image_cache, gate)

    head_block = pl.BlockSpec((1, KEY_HEAD_COUNT, rows, HEAD_WIDTH), lambda r, *_: (r, 0, 0, 0))
    attended = pl.pallas_call(
        functools.partial(relayed_causal_kernel, local, slot),
        grid_spec=pltpu.PrefetchScalarGridSpec(
            num_scalar_prefetch=3,
            grid=(requests,),
            in_specs=[
                head_block,
                pl.BlockSpec((devices, 1, local, width), lambda r, lengths, ranks, first: (0, ranks[r], 0, 0)),
                head_block,
            ],
            out_specs=head_block,
        ),
        out_shape=head_shape,
        compiler_params=pltpu.CompilerParams(vmem_limit_bytes=VMEM_LIMIT),
        name="causal",
    )(lengths, length_rank, first, by_head(queries), kv_all, cross)
    attended = attended.reshape(requests, KEY_HEAD_COUNT, QUERY_PER_KEY, local, HEAD_WIDTH)
    attended = jnp.transpose(attended, (3, 0, 1, 2, 4)).reshape(local, requests, HQ * HEAD_WIDTH)

    length = jnp.sum(jnp.where(owner_slot == rank, lengths, 0))
    own = owned.reshape(slot, width)
    own = jnp.where(jnp.arange(slot, dtype=jnp.int32)[:, None] < length, own, jnp.zeros((), own.dtype))
    kv_cache = jnp.stack([own[:, : width // 2], own[:, width // 2 :]])[:, None]
    return attended, kv_cache


def solution(mesh):
    placed = (
        P("tok", "groups", None),
        P("tok", "groups", None),
        P("tok", "groups", None),
        P("tok", "groups", None),
        P(None, "groups", None, None),
        P(),
        P("groups"),
        P("groups"),
        P("groups"),
    )
    return jax.shard_map(
        relayed if mesh.shape["tok"] == 16 else shards,
        mesh=mesh,
        in_specs=placed,
        out_specs=(P("tok", "groups", None), P(None, ("groups", "tok"), None, None)),
        check_vma=False,
    )
```

```python
import functools
import math

import jax
import jax.numpy as jnp
from jax import lax
from jax.experimental import pallas as pl
from jax.experimental.pallas import tpu as pltpu
from jax.sharding import PartitionSpec as P

HQ = 32
KEY_HEAD_COUNT = 4
HEAD_WIDTH = 128
QUERY_PER_KEY = 8
SCALE = 1.0 / math.sqrt(HEAD_WIDTH)
VMEM_LIMIT = 48 * 1024 * 1024

NT = (((1,), (1,)), ((), ()))


def attend(queries, keys, values, bias):
    scores = lax.dot_general(queries, keys, NT, preferred_element_type=jnp.float32) * SCALE
    if bias is not None:
        scores = scores + bias
    top = jnp.max(scores, axis=-1, keepdims=True)
    weights = jnp.exp(scores - top)
    total = jnp.sum(weights, axis=-1, keepdims=True)
    weighted = jnp.dot(weights.astype(jnp.bfloat16), values, preferred_element_type=jnp.float32)
    return weighted, total


def cross_kernel(local, lengths_ref, image_ref, first_ref, query_ref, cache_ref, gate_ref, out_ref):
    request = pl.program_id(0)
    live = lengths_ref[request] > first_ref[0]

    @pl.when(live)
    def _():
        picture = image_ref[request]
        for group in range(KEY_HEAD_COUNT):
            lanes = slice(group * HEAD_WIDTH, (group + 1) * HEAD_WIDTH)
            weighted, total = attend(
                query_ref[0, group], cache_ref[0, picture, :, lanes], cache_ref[1, picture, :, lanes], None
            )
            out_ref[0, group] = (weighted * (gate_ref[group] / total)).astype(out_ref.dtype)

    @pl.when(jnp.logical_not(live))
    def _():
        out_ref[...] = jnp.zeros_like(out_ref)


def causal_kernel(local, slot, lengths_ref, first_ref, query_ref, kv_ref, cross_ref, out_ref):
    request = pl.program_id(0)
    first = first_ref[0]
    length = lengths_ref[request]
    live = length > first
    rows = QUERY_PER_KEY * local
    needed = first + local

    def run(keys):
        row = lax.broadcasted_iota(jnp.int32, (rows, keys), 0)
        position = first + lax.rem(row, local)
        key = lax.broadcasted_iota(jnp.int32, (rows, keys), 1)
        bias = jnp.where(key <= position, 0.0, -1e30)
        alive = position[:, :HEAD_WIDTH] < length
        for group in range(KEY_HEAD_COUNT):
            lanes = slice(group * HEAD_WIDTH, (group + 1) * HEAD_WIDTH)
            value_lanes = slice((KEY_HEAD_COUNT + group) * HEAD_WIDTH, (KEY_HEAD_COUNT + group + 1) * HEAD_WIDTH)
            weighted, total = attend(
                query_ref[0, group], kv_ref[0, :keys, lanes], kv_ref[0, :keys, value_lanes], bias
            )
            own = (weighted / total).astype(jnp.bfloat16).astype(jnp.float32)
            combined = own + cross_ref[0, group].astype(jnp.float32)
            out_ref[0, group] = jnp.where(alive, combined, 0.0).astype(out_ref.dtype)

    for keys in range(128, slot + 1, 128):
        @pl.when(live & (needed <= keys) & (needed > keys - 128))
        def _():
            run(keys)

    @pl.when(jnp.logical_not(live))
    def _():
        out_ref[...] = jnp.zeros_like(out_ref)


def shards(
    queries,
    cross_query_rows,
    prompt_key_rows,
    prompt_value_rows,
    image_cache,
    query_head_gate,
    lengths,
    owner_slot,
    image_index,
):
    local, requests, _ = queries.shape
    devices = lax.axis_size("tok")
    slot = local * devices
    rank = lax.axis_index("tok")
    rows = QUERY_PER_KEY * local
    first = jnp.full((1,), rank * local, jnp.int32)

    kv = jnp.concatenate([prompt_key_rows, prompt_value_rows], axis=-1)
    gathered = lax.all_gather(kv, "tok", axis=0, tiled=True)
    by_request = jnp.transpose(gathered, (1, 0, 2))

    def by_head(array):
        array = array.reshape(local, requests, KEY_HEAD_COUNT, QUERY_PER_KEY, HEAD_WIDTH)
        return jnp.transpose(array, (1, 2, 3, 0, 4)).reshape(requests, KEY_HEAD_COUNT, rows, HEAD_WIDTH)

    gate = jnp.tanh(query_head_gate).reshape(KEY_HEAD_COUNT, QUERY_PER_KEY, 1)
    gate = jnp.broadcast_to(gate, (KEY_HEAD_COUNT, QUERY_PER_KEY, local)).reshape(KEY_HEAD_COUNT, rows, 1)

    head_block = pl.BlockSpec((1, KEY_HEAD_COUNT, rows, HEAD_WIDTH), lambda r, *_: (r, 0, 0, 0))
    head_shape = jax.ShapeDtypeStruct((requests, KEY_HEAD_COUNT, rows, HEAD_WIDTH), jnp.bfloat16)
    params = pltpu.CompilerParams(vmem_limit_bytes=VMEM_LIMIT)
    flops = requests * HQ * local * HEAD_WIDTH * 4
    cross = pl.pallas_call(
        functools.partial(cross_kernel, local),
        grid_spec=pltpu.PrefetchScalarGridSpec(
            num_scalar_prefetch=3,
            grid=(requests,),
            in_specs=[
                head_block,
                pl.BlockSpec(image_cache.shape, lambda r, *_: (0, 0, 0, 0)),
                pl.BlockSpec(gate.shape, lambda r, *_: (0, 0, 0)),
            ],
            out_specs=head_block,
        ),
        out_shape=head_shape,
        compiler_params=params,
        cost_estimate=pl.CostEstimate(flops=flops * 512, bytes_accessed=8 << 20, transcendentals=0),
        name="cross",
    )(lengths, image_index, first, by_head(cross_query_rows), image_cache, gate)

    attended = pl.pallas_call(
        functools.partial(causal_kernel, local, slot),
        grid_spec=pltpu.PrefetchScalarGridSpec(
            num_scalar_prefetch=2,
            grid=(requests,),
            in_specs=[
                head_block,
                pl.BlockSpec((1, slot, 2 * KEY_HEAD_COUNT * HEAD_WIDTH), lambda r, *_: (r, 0, 0)),
                head_block,
            ],
            out_specs=head_block,
        ),
        out_shape=head_shape,
        compiler_params=params,
        cost_estimate=pl.CostEstimate(flops=flops * slot, bytes_accessed=24 << 20, transcendentals=0),
        name="causal",
    )(lengths, first, by_head(queries), by_request, cross)
    attended = attended.reshape(requests, KEY_HEAD_COUNT, QUERY_PER_KEY, local, HEAD_WIDTH)
    attended = jnp.transpose(attended, (3, 0, 1, 2, 4)).reshape(local, requests, HQ * HEAD_WIDTH)

    own_request = jnp.argmax(owner_slot == rank).astype(jnp.int32)
    length = lax.dynamic_index_in_dim(lengths, own_request, 0, keepdims=False)
    own = lax.dynamic_index_in_dim(by_request, own_request, 0, keepdims=False)
    own = jnp.where(jnp.arange(slot, dtype=jnp.int32)[:, None] < length, own, jnp.zeros((), own.dtype))
    width = KEY_HEAD_COUNT * HEAD_WIDTH
    kv_cache = jnp.stack([own[:, :width], own[:, width:]])[:, None]
    return attended, kv_cache


CHUNK = 8
STEP_US = 1.5
LINK_BYTES_PER_US = 45000.0
SCALE_LOG2 = SCALE * math.log2(math.e)


def rank_limit(requests, slot, first):
    if first == 0:
        return requests
    return min(requests, (requests * slot // 2 - requests) // first)


def relay_plan(chips, requests, slot, local):
    span = slot // chips
    limit = [rank_limit(requests, slot, span * chip) for chip in range(chips)]
    chunks = [(0, CHUNK), (CHUNK, requests)]

    def ranks(chip, chunk, up):
        lo, hi = chunks[chunk]
        top = limit[chip - chip % 2] if up else limit[chip]
        return lo, max(lo, min(hi, top))

    free = {}
    rate = local * 2048 / LINK_BYTES_PER_US
    pending = []
    for chip in range(chips):
        pending.append((0.0, chip, chip, "own", 0))
        pending.append((rate * CHUNK * (chip // 2 + 1), chip, chip, "own", 1))
    events = [[] for _ in range(chips)]
    while pending:
        pending.sort()
        time, chip, source, via, chunk = pending.pop(0)
        sends = []
        if via != "side":
            if chip + 2 < chips:
                sends.append((chip + 2, "up"))
            if source < (chip ^ 1):
                sends.append((chip ^ 1, "side"))
        kept = []
        for target, way in sends:
            lo, hi = ranks(target, chunk, way == "up")
            if hi > lo:
                start = max(time, free.get((chip, target), 0.0))
                end = start + rate * (hi - lo)
                free[chip, target] = end
                pending.append((end + 1.0, target, source, way, chunk))
                kept.append((target, lo, hi))
        got = ranks(chip, chunk, via == "up")
        need = ranks(chip, chunk, False)
        events[chip].append((time, source, via, chunk, got, need, kept))

    cross_steps, causal_steps = [], []
    for chip in range(chips):
        last = max(position for position, event in enumerate(events[chip]) if event[3] == 0)
        early, late = {}, {}
        base = max(limit[chip], int(events[chip][last][0] / STEP_US) + 1)
        for position, event in enumerate(events[chip]):
            step = int(event[0] / STEP_US)
            if step < limit[chip]:
                early.setdefault(step, []).append(position)
            elif position <= last:
                late.setdefault(0, []).append(position)
            else:
                late.setdefault(max(0, min(CHUNK, step - base)), []).append(position)
        cross_steps.append(early)
        causal_steps.append(late)
    return limit, events, cross_steps, causal_steps


def weigh(scores, values):
    top = jnp.max(scores, axis=-1, keepdims=True)
    weights = jnp.exp2((scores - top) * SCALE_LOG2)
    total = jnp.sum(weights, axis=-1, keepdims=True)
    return jnp.dot(weights.astype(jnp.bfloat16), values, preferred_element_type=jnp.float32), total


def relay_kernel(
    devices, requests, local, slot, plan,
    order_ref, image_ref, lengths_ref, picks_ref, query_ref, cross_query_ref, cache_ref, gate_ref,
    out_ref, owned_ref, kv_ref, send_sem, recv_sem, pass_sem, owned_send, owned_recv, local_sem,
):
    limit, events, cross_steps, causal_steps = plan
    me = lax.axis_index("tok")
    chip, core = lax.div(me, 2), lax.rem(me, 2)
    rows = QUERY_PER_KEY * local
    first = me * local
    needed = first + local
    barrier = pltpu.get_barrier_semaphore()

    def greet(offset, carry):
        pl.semaphore_signal(
            barrier, inc=1, device_id={"tok": lax.rem(me + offset, devices)}, device_id_type=pl.DeviceIdType.MESH
        )
        return carry

    lax.fori_loop(1, devices, greet, 0)
    pl.semaphore_wait(barrier, devices - 1)

    keep = pltpu.make_async_copy(picks_ref.at[pl.ds(0, requests)], kv_ref.at[me], local_sem.at[0])
    keep_owned = pltpu.make_async_copy(picks_ref.at[requests + me], owned_ref.at[me], local_sem.at[1])

    def relay(source, lo, hi, chunk, target, send, own):
        here = picks_ref.at[pl.ds(lo, hi - lo)] if own else kv_ref.at[source, pl.ds(lo, hi - lo)]
        return pltpu.make_async_remote_copy(
            src_ref=here,
            dst_ref=kv_ref.at[source, pl.ds(lo, hi - lo)],
            send_sem=send,
            recv_sem=recv_sem.at[2 * source + chunk],
            device_id={"tok": target},
            device_id_type=pl.DeviceIdType.MESH,
        )

    def copies(number, position):
        _, source_chip, via, chunk, _, need, sends = events[number][position]
        source = 2 * source_chip + core
        result = []
        for index, (target, lo, hi) in enumerate(sends):
            result.append(
                relay(source, lo, hi, chunk, 2 * target + core, send_sem.at[index, 2 * source_chip + chunk], via == "own")
            )
        if need[1] > need[0]:
            result.append(
                relay(source, need[0], need[1], chunk, 2 * number + 1 - core, pass_sem.at[2 * source_chip + chunk], via == "own")
            )
        return result

    def handle(number, position):
        _, source_chip, via, chunk, got, _, _ = events[number][position]
        if via != "own":
            relay(2 * source_chip + core, got[0], got[1], chunk, me, pass_sem.at[0], False).wait_recv()
        for copy in copies(number, position):
            copy.start()

    def wait_passed(number, wanted):
        for _, source_chip, _, chunk, _, need, _ in events[number]:
            if chunk == wanted and need[1] > need[0]:
                relay(2 * source_chip + 1 - core, need[0], need[1], chunk, me, pass_sem.at[0], False).wait_recv()

    def owned_copy(offset):
        target = lax.rem(me + offset, devices)
        return pltpu.make_async_remote_copy(
            src_ref=picks_ref.at[requests + target],
            dst_ref=owned_ref.at[me],
            send_sem=owned_send.at[offset],
            recv_sem=owned_recv.at[offset],
            device_id={"tok": target},
            device_id_type=pl.DeviceIdType.MESH,
        )

    def owned_start(offset, carry):
        owned_copy(offset).start()
        return carry

    count = limit[0]
    for number in range(1, devices // 2):
        count = jnp.where(chip == number, limit[number], count)

    def events_at(steps, step, last):
        for number in range(devices // 2):
            @pl.when(chip == number)
            def _():
                for when in sorted(set(steps[number]) | set(last)):
                    @pl.when(step == when)
                    def _():
                        for position in steps[number].get(when, ()):
                            handle(number, position)
                        if when in last:
                            wait_passed(number, last[when])

    def cross_step(place, carry):
        events_at(cross_steps, place, {})

        @pl.when(place == 0)
        def _():
            keep.start()
            keep_owned.start()
            lax.fori_loop(devices - me, devices, owned_start, 0)

        request = order_ref[place]
        picture = image_ref[request]
        for group in range(KEY_HEAD_COUNT):
            lanes = slice(group * HEAD_WIDTH, (group + 1) * HEAD_WIDTH)
            scores = lax.dot_general(
                cross_query_ref[request, group], cache_ref[0, picture, :, lanes], NT, preferred_element_type=jnp.float32
            )
            weighted, total = weigh(scores, cache_ref[1, picture, :, lanes])
            out_ref[place, group] = (weighted * (gate_ref[group] / total)).astype(out_ref.dtype)
        return carry

    lax.fori_loop(0, count, cross_step, 0)
    keep.wait()

    def run(place, keys):
        request = order_ref[place]
        sources = -(-keys // local)
        row = lax.broadcasted_iota(jnp.int32, (rows, keys), 0)
        position = first + lax.rem(row, local)
        key = lax.broadcasted_iota(jnp.int32, (rows, keys), 1)
        allowed = key <= position
        alive = position[:, :HEAD_WIDTH] < lengths_ref[request]
        written = lax.broadcasted_iota(jnp.int32, (keys, HEAD_WIDTH), 0) < needed

        def rows_of(lane_block):
            lanes = slice(lane_block * HEAD_WIDTH, (lane_block + 1) * HEAD_WIDTH)
            pieces = kv_ref[:sources, place, :, lanes].astype(jnp.float32)
            return pieces.reshape(sources * local, HEAD_WIDTH)[:keys]

        for group in range(KEY_HEAD_COUNT):
            key_rows = rows_of(group).astype(jnp.bfloat16)
            value_rows = jnp.where(written, rows_of(KEY_HEAD_COUNT + group), 0.0).astype(jnp.bfloat16)
            scores = lax.dot_general(query_ref[request, group], key_rows, NT, preferred_element_type=jnp.float32)
            weighted, total = weigh(jnp.where(allowed, scores, -1e30), value_rows)
            own = (weighted / total).astype(jnp.bfloat16).astype(jnp.float32)
            combined = own + out_ref[place, group].astype(jnp.float32)
            out_ref[place, group] = jnp.where(alive, combined, 0.0).astype(out_ref.dtype)

    def causal_step(place, carry):
        events_at(causal_steps, place, {0: 0, CHUNK: 1})

        @pl.when(place == CHUNK)
        def _():
            lax.fori_loop(1, devices - me, owned_start, 0)

        for keys in range(128, slot + 1, 128):
            @pl.when((needed <= keys) & (needed > keys - 128))
            def _():
                run(place, keys)

        return carry

    lax.fori_loop(0, count, causal_step, 0)

    def clear(place, carry):
        out_ref[place] = jnp.zeros(out_ref.shape[1:], out_ref.dtype)
        return carry

    lax.fori_loop(count, requests, clear, 0)

    for number in range(devices // 2):
        @pl.when(chip == number)
        def _():
            for position in range(len(events[number])):
                for copy in copies(number, position):
                    copy.wait_send()

    def owned_wait(offset, carry):
        source = lax.rem(me + devices - offset, devices)
        pltpu.make_async_remote_copy(
            src_ref=picks_ref.at[requests + me],
            dst_ref=owned_ref.at[source],
            send_sem=owned_send.at[offset],
            recv_sem=owned_recv.at[offset],
            device_id={"tok": source},
            device_id_type=pl.DeviceIdType.MESH,
        ).wait_recv()
        owned_copy(offset).wait_send()
        return carry

    lax.fori_loop(1, devices, owned_wait, 0)
    keep_owned.wait()


def relayed(
    queries,
    cross_query_rows,
    prompt_key_rows,
    prompt_value_rows,
    image_cache,
    query_head_gate,
    lengths,
    owner_slot,
    image_index,
):
    local, requests, _ = queries.shape
    devices = lax.axis_size("tok")
    slot = local * devices
    rank = lax.axis_index("tok")
    rows = QUERY_PER_KEY * local
    width = 2 * KEY_HEAD_COUNT * HEAD_WIDTH
    first = jnp.full((1,), rank * local, jnp.int32)
    ids = jnp.arange(requests, dtype=jnp.int32)

    longer = lengths[None, :] > lengths[:, None]
    tied = (lengths[None, :] == lengths[:, None]) & (ids[None, :] < ids[:, None])
    length_rank = jnp.sum((longer | tied).astype(jnp.int32), axis=1)
    chosen = jnp.concatenate([length_rank, owner_slot + requests]).reshape(2, requests)
    places = jnp.arange(2 * requests, dtype=jnp.int32)
    pick = (places[:, None, None] == chosen[None]).any(axis=1).astype(jnp.bfloat16)
    kv = jnp.concatenate([prompt_key_rows, prompt_value_rows], axis=-1)
    picks = jnp.einsum("sr,lrd->sld", pick, kv, preferred_element_type=jnp.float32).astype(jnp.bfloat16)

    def by_head(array):
        array = array.reshape(local, requests, KEY_HEAD_COUNT, QUERY_PER_KEY, HEAD_WIDTH)
        return jnp.transpose(array, (1, 2, 3, 0, 4)).reshape(requests, KEY_HEAD_COUNT, rows, HEAD_WIDTH)

    gate = jnp.tanh(query_head_gate).reshape(KEY_HEAD_COUNT, QUERY_PER_KEY, 1)
    gate = jnp.broadcast_to(gate, (KEY_HEAD_COUNT, QUERY_PER_KEY, local)).reshape(KEY_HEAD_COUNT, rows, 1)

    head_shape = jax.ShapeDtypeStruct((requests, KEY_HEAD_COUNT, rows, HEAD_WIDTH), jnp.bfloat16)
    anywhere = pl.BlockSpec(memory_space=pl.ANY)
    vmem = pl.BlockSpec(memory_space=pltpu.VMEM)
    plan = relay_plan(devices // 2, requests, slot, local)
    order = jnp.sum(ids[:, None] * (length_rank[:, None] == ids[None, :]), axis=0).astype(jnp.int32)
    smem = pl.BlockSpec(memory_space=pltpu.SMEM)
    by_rank, owned = pl.pallas_call(
        functools.partial(relay_kernel, devices, requests, local, slot, plan),
        in_specs=[smem, smem, smem, vmem, vmem, vmem, vmem, vmem],
        out_specs=[vmem, anywhere],
        out_shape=[head_shape, jax.ShapeDtypeStruct((devices, local, width), jnp.bfloat16)],
        scratch_shapes=[
            pltpu.VMEM((devices, requests, local, width), jnp.bfloat16),
            pltpu.SemaphoreType.DMA((2, devices)),
            pltpu.SemaphoreType.DMA((2 * devices,)),
            pltpu.SemaphoreType.DMA((devices,)),
            pltpu.SemaphoreType.DMA((devices,)),
            pltpu.SemaphoreType.DMA((devices,)),
            pltpu.SemaphoreType.DMA((2,)),
        ],
        compiler_params=pltpu.CompilerParams(
            collective_id=0, has_side_effects=True, vmem_limit_bytes=VMEM_LIMIT
        ),
        name="relay_attention",
    )(order, image_index, lengths, picks, by_head(queries), by_head(cross_query_rows), image_cache, gate)
    attended = jnp.take(by_rank, length_rank, axis=0)
    attended = attended.reshape(requests, KEY_HEAD_COUNT, QUERY_PER_KEY, local, HEAD_WIDTH)
    attended = jnp.transpose(attended, (3, 0, 1, 2, 4)).reshape(local, requests, HQ * HEAD_WIDTH)

    length = jnp.sum(jnp.where(owner_slot == rank, lengths, 0))
    own = owned.reshape(slot, width)
    own = jnp.where(jnp.arange(slot, dtype=jnp.int32)[:, None] < length, own, jnp.zeros((), own.dtype))
    kv_cache = jnp.stack([own[:, : width // 2], own[:, width // 2 :]])[:, None]
    return attended, kv_cache


def solution(mesh):
    placed = (
        P("tok", "groups", None),
        P("tok", "groups", None),
        P("tok", "groups", None),
        P("tok", "groups", None),
        P(None, "groups", None, None),
        P(),
        P("groups"),
        P("groups"),
        P("groups"),
    )
    return jax.shard_map(
        relayed if mesh.shape["tok"] == 16 else shards,
        mesh=mesh,
        in_specs=placed,
        out_specs=(P("tok", "groups", None), P(None, ("groups", "tok"), None, None)),
        check_vma=False,
    )
```

```python
import functools
import math

import jax
import jax.numpy as jnp
from jax import lax
from jax.experimental import pallas as pl
from jax.experimental.pallas import tpu as pltpu
from jax.sharding import PartitionSpec as P

HQ = 32
KEY_HEAD_COUNT = 4
HEAD_WIDTH = 128
QUERY_PER_KEY = 8
SCALE = 1.0 / math.sqrt(HEAD_WIDTH)
VMEM_LIMIT = 52 * 1024 * 1024

NT = (((1,), (1,)), ((), ()))


def attend(queries, keys, values, bias):
    scores = lax.dot_general(queries, keys, NT, preferred_element_type=jnp.float32) * SCALE
    if bias is not None:
        scores = scores + bias
    top = jnp.max(scores, axis=-1, keepdims=True)
    weights = jnp.exp(scores - top)
    total = jnp.sum(weights, axis=-1, keepdims=True)
    weighted = jnp.dot(weights.astype(jnp.bfloat16), values, preferred_element_type=jnp.float32)
    return weighted, total


def cross_kernel(local, lengths_ref, image_ref, first_ref, query_ref, cache_ref, gate_ref, out_ref):
    request = pl.program_id(0)
    live = lengths_ref[request] > first_ref[0]

    @pl.when(live)
    def _():
        picture = image_ref[request]
        for group in range(KEY_HEAD_COUNT):
            lanes = slice(group * HEAD_WIDTH, (group + 1) * HEAD_WIDTH)
            weighted, total = attend(
                query_ref[0, group], cache_ref[0, picture, :, lanes], cache_ref[1, picture, :, lanes], None
            )
            out_ref[0, group] = (weighted * (gate_ref[group] / total)).astype(out_ref.dtype)

    @pl.when(jnp.logical_not(live))
    def _():
        out_ref[...] = jnp.zeros_like(out_ref)


def causal_kernel(local, slot, lengths_ref, first_ref, query_ref, kv_ref, cross_ref, out_ref):
    request = pl.program_id(0)
    first = first_ref[0]
    length = lengths_ref[request]
    live = length > first
    rows = QUERY_PER_KEY * local
    needed = first + local

    def run(keys):
        row = lax.broadcasted_iota(jnp.int32, (rows, keys), 0)
        position = first + lax.rem(row, local)
        key = lax.broadcasted_iota(jnp.int32, (rows, keys), 1)
        bias = jnp.where(key <= position, 0.0, -1e30)
        alive = position[:, :HEAD_WIDTH] < length
        for group in range(KEY_HEAD_COUNT):
            lanes = slice(group * HEAD_WIDTH, (group + 1) * HEAD_WIDTH)
            value_lanes = slice((KEY_HEAD_COUNT + group) * HEAD_WIDTH, (KEY_HEAD_COUNT + group + 1) * HEAD_WIDTH)
            weighted, total = attend(
                query_ref[0, group], kv_ref[0, :keys, lanes], kv_ref[0, :keys, value_lanes], bias
            )
            own = (weighted / total).astype(jnp.bfloat16).astype(jnp.float32)
            combined = own + cross_ref[0, group].astype(jnp.float32)
            out_ref[0, group] = jnp.where(alive, combined, 0.0).astype(out_ref.dtype)

    for keys in range(128, slot + 1, 128):
        @pl.when(live & (needed <= keys) & (needed > keys - 128))
        def _():
            run(keys)

    @pl.when(jnp.logical_not(live))
    def _():
        out_ref[...] = jnp.zeros_like(out_ref)


def shards(
    queries,
    cross_query_rows,
    prompt_key_rows,
    prompt_value_rows,
    image_cache,
    query_head_gate,
    lengths,
    owner_slot,
    image_index,
):
    local, requests, _ = queries.shape
    devices = lax.axis_size("tok")
    slot = local * devices
    rank = lax.axis_index("tok")
    rows = QUERY_PER_KEY * local
    first = jnp.full((1,), rank * local, jnp.int32)

    kv = jnp.concatenate([prompt_key_rows, prompt_value_rows], axis=-1)
    gathered = lax.all_gather(kv, "tok", axis=0, tiled=True)
    by_request = jnp.transpose(gathered, (1, 0, 2))

    def by_head(array):
        array = array.reshape(local, requests, KEY_HEAD_COUNT, QUERY_PER_KEY, HEAD_WIDTH)
        return jnp.transpose(array, (1, 2, 3, 0, 4)).reshape(requests, KEY_HEAD_COUNT, rows, HEAD_WIDTH)

    gate = jnp.tanh(query_head_gate).reshape(KEY_HEAD_COUNT, QUERY_PER_KEY, 1)
    gate = jnp.broadcast_to(gate, (KEY_HEAD_COUNT, QUERY_PER_KEY, local)).reshape(KEY_HEAD_COUNT, rows, 1)

    head_block = pl.BlockSpec((1, KEY_HEAD_COUNT, rows, HEAD_WIDTH), lambda r, *_: (r, 0, 0, 0))
    head_shape = jax.ShapeDtypeStruct((requests, KEY_HEAD_COUNT, rows, HEAD_WIDTH), jnp.bfloat16)
    params = pltpu.CompilerParams(vmem_limit_bytes=VMEM_LIMIT)
    flops = requests * HQ * local * HEAD_WIDTH * 4
    cross = pl.pallas_call(
        functools.partial(cross_kernel, local),
        grid_spec=pltpu.PrefetchScalarGridSpec(
            num_scalar_prefetch=3,
            grid=(requests,),
            in_specs=[
                head_block,
                pl.BlockSpec(image_cache.shape, lambda r, *_: (0, 0, 0, 0)),
                pl.BlockSpec(gate.shape, lambda r, *_: (0, 0, 0)),
            ],
            out_specs=head_block,
        ),
        out_shape=head_shape,
        compiler_params=params,
        cost_estimate=pl.CostEstimate(flops=flops * 512, bytes_accessed=8 << 20, transcendentals=0),
        name="cross",
    )(lengths, image_index, first, by_head(cross_query_rows), image_cache, gate)

    attended = pl.pallas_call(
        functools.partial(causal_kernel, local, slot),
        grid_spec=pltpu.PrefetchScalarGridSpec(
            num_scalar_prefetch=2,
            grid=(requests,),
            in_specs=[
                head_block,
                pl.BlockSpec((1, slot, 2 * KEY_HEAD_COUNT * HEAD_WIDTH), lambda r, *_: (r, 0, 0)),
                head_block,
            ],
            out_specs=head_block,
        ),
        out_shape=head_shape,
        compiler_params=params,
        cost_estimate=pl.CostEstimate(flops=flops * slot, bytes_accessed=24 << 20, transcendentals=0),
        name="causal",
    )(lengths, first, by_head(queries), by_request, cross)
    attended = attended.reshape(requests, KEY_HEAD_COUNT, QUERY_PER_KEY, local, HEAD_WIDTH)
    attended = jnp.transpose(attended, (3, 0, 1, 2, 4)).reshape(local, requests, HQ * HEAD_WIDTH)

    own_request = jnp.argmax(owner_slot == rank).astype(jnp.int32)
    length = lax.dynamic_index_in_dim(lengths, own_request, 0, keepdims=False)
    own = lax.dynamic_index_in_dim(by_request, own_request, 0, keepdims=False)
    own = jnp.where(jnp.arange(slot, dtype=jnp.int32)[:, None] < length, own, jnp.zeros((), own.dtype))
    width = KEY_HEAD_COUNT * HEAD_WIDTH
    kv_cache = jnp.stack([own[:, :width], own[:, width:]])[:, None]
    return attended, kv_cache


CHUNK = 8
STEP_US = 1.5
TURN_STEPS = 8
LINK_BYTES_PER_US = 45000.0
SCALE_LOG2 = SCALE * math.log2(math.e)


def rank_limit(requests, slot, first):
    if first == 0:
        return requests
    return min(requests, (requests * slot // 2 - requests) // first)


def relay_plan(chips, requests, slot, local):
    span = slot // chips
    limit = [rank_limit(requests, slot, span * chip) for chip in range(chips)]
    chunks = [(0, CHUNK), (CHUNK, requests)]

    def ranks(chip, chunk, up):
        lo, hi = chunks[chunk]
        top = limit[chip - chip % 2] if up else limit[chip]
        return lo, max(lo, min(hi, top))

    free = {}
    rate = local * 2048 / LINK_BYTES_PER_US
    pending = []
    for chip in range(chips):
        pending.append((0.0, chip, chip, "own", 0))
        pending.append((rate * CHUNK * (chip // 2 + 1), chip, chip, "own", 1))
    events = [[] for _ in range(chips)]
    while pending:
        pending.sort()
        time, chip, source, via, chunk = pending.pop(0)
        sends = []
        if via != "side":
            if chip + 2 < chips:
                sends.append((chip + 2, "up"))
            if source < (chip ^ 1):
                sends.append((chip ^ 1, "side"))
        kept = []
        for target, way in sends:
            lo, hi = ranks(target, chunk, way == "up")
            if hi > lo:
                start = max(time, free.get((chip, target), 0.0))
                end = start + rate * (hi - lo)
                free[chip, target] = end
                pending.append((end + 1.0, target, source, way, chunk))
                kept.append((target, lo, hi))
        got = ranks(chip, chunk, via == "up")
        need = ranks(chip, chunk, False)
        events[chip].append((time, source, via, chunk, got, need, kept))

    cross_steps, causal_steps = [], []
    for chip in range(chips):
        last = max(position for position, event in enumerate(events[chip]) if event[3] == 0)
        early, late = {}, {}
        base = max(limit[chip], int(events[chip][last][0] / STEP_US) + 1)
        for position, event in enumerate(events[chip]):
            step = int(event[0] / STEP_US)
            if step < limit[chip]:
                early.setdefault(step, []).append(position)
            elif position <= last:
                late.setdefault(0, []).append(position)
            else:
                late.setdefault(max(0, min(CHUNK, step - base)), []).append(position)
        cross_steps.append(early)
        causal_steps.append(late)
    return limit, events, cross_steps, causal_steps


def weigh(scores, values):
    top = jnp.max(scores, axis=-1, keepdims=True)
    weights = jnp.exp2((scores - top) * SCALE_LOG2)
    total = jnp.sum(weights, axis=-1, keepdims=True)
    return jnp.dot(weights.astype(jnp.bfloat16), values, preferred_element_type=jnp.float32), total


def relay_kernel(
    devices, requests, local, slot, plan,
    order_ref, image_ref, lengths_ref, picks_ref, query_ref, cross_query_ref, cache_ref, gate_ref,
    out_ref, owned_ref, kv_ref, turned_ref, turned_cross_ref, send_sem, recv_sem, pass_sem, owned_send, owned_recv, local_sem,
):
    limit, events, cross_steps, causal_steps = plan
    me = lax.axis_index("tok")
    chip, core = lax.div(me, 2), lax.rem(me, 2)
    rows = QUERY_PER_KEY * local
    first = me * local
    needed = first + local
    barrier = pltpu.get_barrier_semaphore()

    def greet(offset, carry):
        pl.semaphore_signal(
            barrier, inc=1, device_id={"tok": lax.rem(me + offset, devices)}, device_id_type=pl.DeviceIdType.MESH
        )
        return carry

    lax.fori_loop(1, devices, greet, 0)
    pl.semaphore_wait(barrier, devices - 1)

    keep = pltpu.make_async_copy(picks_ref.at[pl.ds(0, requests)], kv_ref.at[me], local_sem.at[0])
    keep_owned = pltpu.make_async_copy(picks_ref.at[requests + me], owned_ref.at[me], local_sem.at[1])

    def relay(source, lo, hi, chunk, target, send, own):
        here = picks_ref.at[pl.ds(lo, hi - lo)] if own else kv_ref.at[source, pl.ds(lo, hi - lo)]
        return pltpu.make_async_remote_copy(
            src_ref=here,
            dst_ref=kv_ref.at[source, pl.ds(lo, hi - lo)],
            send_sem=send,
            recv_sem=recv_sem.at[2 * source + chunk],
            device_id={"tok": target},
            device_id_type=pl.DeviceIdType.MESH,
        )

    def copies(number, position):
        _, source_chip, via, chunk, _, need, sends = events[number][position]
        source = 2 * source_chip + core
        result = []
        for index, (target, lo, hi) in enumerate(sends):
            result.append(
                relay(source, lo, hi, chunk, 2 * target + core, send_sem.at[index, 2 * source_chip + chunk], via == "own")
            )
        if need[1] > need[0]:
            result.append(
                relay(source, need[0], need[1], chunk, 2 * number + 1 - core, pass_sem.at[2 * source_chip + chunk], via == "own")
            )
        return result

    def handle(number, position):
        _, source_chip, via, chunk, got, _, _ = events[number][position]
        if via != "own":
            relay(2 * source_chip + core, got[0], got[1], chunk, me, pass_sem.at[0], False).wait_recv()
        for copy in copies(number, position):
            copy.start()

    def wait_passed(number, wanted):
        for _, source_chip, _, chunk, _, need, _ in events[number]:
            if chunk == wanted and need[1] > need[0]:
                relay(2 * source_chip + 1 - core, need[0], need[1], chunk, me, pass_sem.at[0], False).wait_recv()

    def owned_copy(offset):
        target = lax.rem(me + offset, devices)
        return pltpu.make_async_remote_copy(
            src_ref=picks_ref.at[requests + target],
            dst_ref=owned_ref.at[me],
            send_sem=owned_send.at[offset],
            recv_sem=owned_recv.at[offset],
            device_id={"tok": target},
            device_id_type=pl.DeviceIdType.MESH,
        )

    def owned_start(offset, carry):
        owned_copy(offset).start()
        return carry

    count = limit[0]
    for number in range(1, devices // 2):
        count = jnp.where(chip == number, limit[number], count)

    def events_at(steps, step, last):
        for number in range(devices // 2):
            @pl.when(chip == number)
            def _():
                for when in sorted(set(steps[number]) | set(last)):
                    @pl.when(step == when)
                    def _():
                        for position in steps[number].get(when, ()):
                            handle(number, position)
                        if when in last:
                            wait_passed(number, last[when])

    def turn(source_ref, target_ref, head):
        lanes = pl.ds(pl.multiple_of(head * HEAD_WIDTH, HEAD_WIDTH), HEAD_WIDTH)
        target_ref[:, head] = jnp.swapaxes(source_ref[:, :, lanes].astype(jnp.float32), 0, 1)

    def turn_cross(head, carry):
        turn(cross_query_ref, turned_cross_ref, head)
        return carry

    def turn_own(head, carry):
        turn(query_ref, turned_ref, head)
        return carry

    def head_rows(turned, request, group):
        part = turned[request, group * QUERY_PER_KEY : (group + 1) * QUERY_PER_KEY]
        return part.reshape(rows, HEAD_WIDTH).astype(jnp.bfloat16)

    def cross_step(place, carry):
        events_at(cross_steps, place, {})

        @pl.when(place == 0)
        def _():
            keep.start()
            keep_owned.start()
            lax.fori_loop(devices - me, devices, owned_start, 0)
            lax.fori_loop(0, HQ, turn_cross, 0)

        @pl.when(place < TURN_STEPS)
        def _():
            lax.fori_loop(place * (HQ // TURN_STEPS), (place + 1) * (HQ // TURN_STEPS), turn_own, 0)

        request = order_ref[place]
        picture = image_ref[request]
        for group in range(KEY_HEAD_COUNT):
            lanes = slice(group * HEAD_WIDTH, (group + 1) * HEAD_WIDTH)
            scores = lax.dot_general(
                head_rows(turned_cross_ref, request, group), cache_ref[0, picture, :, lanes], NT, preferred_element_type=jnp.float32
            )
            weighted, total = weigh(scores, cache_ref[1, picture, :, lanes])
            out_ref[place, group] = (weighted * (gate_ref[group] / total)).astype(out_ref.dtype)
        return carry

    lax.fori_loop(0, count, cross_step, 0)
    keep.wait()

    def run(place, keys):
        request = order_ref[place]
        sources = -(-keys // local)
        row = lax.broadcasted_iota(jnp.int32, (rows, keys), 0)
        position = first + lax.rem(row, local)
        key = lax.broadcasted_iota(jnp.int32, (rows, keys), 1)
        allowed = key <= position
        alive = position[:, :HEAD_WIDTH] < lengths_ref[request]
        written = lax.broadcasted_iota(jnp.int32, (keys, HEAD_WIDTH), 0) < needed

        def rows_of(lane_block):
            lanes = slice(lane_block * HEAD_WIDTH, (lane_block + 1) * HEAD_WIDTH)
            pieces = kv_ref[:sources, place, :, lanes].astype(jnp.float32)
            return pieces.reshape(sources * local, HEAD_WIDTH)[:keys]

        for group in range(KEY_HEAD_COUNT):
            key_rows = rows_of(group).astype(jnp.bfloat16)
            value_rows = jnp.where(written, rows_of(KEY_HEAD_COUNT + group), 0.0).astype(jnp.bfloat16)
            scores = lax.dot_general(
                head_rows(turned_ref, request, group), key_rows, NT, preferred_element_type=jnp.float32
            )
            weighted, total = weigh(jnp.where(allowed, scores, -1e30), value_rows)
            own = (weighted / total).astype(jnp.bfloat16).astype(jnp.float32)
            combined = own + out_ref[place, group].astype(jnp.float32)
            out_ref[place, group] = jnp.where(alive, combined, 0.0).astype(out_ref.dtype)

    def causal_step(place, carry):
        events_at(causal_steps, place, {0: 0, CHUNK: 1})

        @pl.when(place == CHUNK)
        def _():
            lax.fori_loop(1, devices - me, owned_start, 0)

        for keys in range(128, slot + 1, 128):
            @pl.when((needed <= keys) & (needed > keys - 128))
            def _():
                run(place, keys)

        return carry

    lax.fori_loop(0, count, causal_step, 0)

    def clear(place, carry):
        out_ref[place] = jnp.zeros(out_ref.shape[1:], out_ref.dtype)
        return carry

    lax.fori_loop(count, requests, clear, 0)

    for number in range(devices // 2):
        @pl.when(chip == number)
        def _():
            for position in range(len(events[number])):
                for copy in copies(number, position):
                    copy.wait_send()

    def owned_wait(offset, carry):
        source = lax.rem(me + devices - offset, devices)
        pltpu.make_async_remote_copy(
            src_ref=picks_ref.at[requests + me],
            dst_ref=owned_ref.at[source],
            send_sem=owned_send.at[offset],
            recv_sem=owned_recv.at[offset],
            device_id={"tok": source},
            device_id_type=pl.DeviceIdType.MESH,
        ).wait_recv()
        owned_copy(offset).wait_send()
        return carry

    lax.fori_loop(1, devices, owned_wait, 0)
    keep_owned.wait()


def relayed(
    queries,
    cross_query_rows,
    prompt_key_rows,
    prompt_value_rows,
    image_cache,
    query_head_gate,
    lengths,
    owner_slot,
    image_index,
):
    local, requests, _ = queries.shape
    devices = lax.axis_size("tok")
    slot = local * devices
    rank = lax.axis_index("tok")
    rows = QUERY_PER_KEY * local
    width = 2 * KEY_HEAD_COUNT * HEAD_WIDTH
    first = jnp.full((1,), rank * local, jnp.int32)
    ids = jnp.arange(requests, dtype=jnp.int32)

    longer = lengths[None, :] > lengths[:, None]
    tied = (lengths[None, :] == lengths[:, None]) & (ids[None, :] < ids[:, None])
    length_rank = jnp.sum((longer | tied).astype(jnp.int32), axis=1)
    chosen = jnp.concatenate([length_rank, owner_slot + requests]).reshape(2, requests)
    places = jnp.arange(2 * requests, dtype=jnp.int32)
    pick = (places[:, None, None] == chosen[None]).any(axis=1).astype(jnp.bfloat16)
    kv = jnp.concatenate([prompt_key_rows, prompt_value_rows], axis=-1)
    picks = jnp.einsum("sr,lrd->sld", pick, kv, preferred_element_type=jnp.float32).astype(jnp.bfloat16)

    gate = jnp.tanh(query_head_gate).reshape(KEY_HEAD_COUNT, QUERY_PER_KEY, 1)
    gate = jnp.broadcast_to(gate, (KEY_HEAD_COUNT, QUERY_PER_KEY, local)).reshape(KEY_HEAD_COUNT, rows, 1)

    head_shape = jax.ShapeDtypeStruct((requests, KEY_HEAD_COUNT, rows, HEAD_WIDTH), jnp.bfloat16)
    anywhere = pl.BlockSpec(memory_space=pl.ANY)
    vmem = pl.BlockSpec(memory_space=pltpu.VMEM)
    plan = relay_plan(devices // 2, requests, slot, local)
    order = jnp.sum(ids[:, None] * (length_rank[:, None] == ids[None, :]), axis=0).astype(jnp.int32)
    smem = pl.BlockSpec(memory_space=pltpu.SMEM)
    by_rank, owned = pl.pallas_call(
        functools.partial(relay_kernel, devices, requests, local, slot, plan),
        in_specs=[smem, smem, smem, vmem, vmem, vmem, vmem, vmem],
        out_specs=[vmem, anywhere],
        out_shape=[head_shape, jax.ShapeDtypeStruct((devices, local, width), jnp.bfloat16)],
        scratch_shapes=[
            pltpu.VMEM((devices, requests, local, width), jnp.bfloat16),
            pltpu.VMEM((requests, HQ, local, HEAD_WIDTH), jnp.float32),
            pltpu.VMEM((requests, HQ, local, HEAD_WIDTH), jnp.float32),
            pltpu.SemaphoreType.DMA((2, devices)),
            pltpu.SemaphoreType.DMA((2 * devices,)),
            pltpu.SemaphoreType.DMA((devices,)),
            pltpu.SemaphoreType.DMA((devices,)),
            pltpu.SemaphoreType.DMA((devices,)),
            pltpu.SemaphoreType.DMA((2,)),
        ],
        compiler_params=pltpu.CompilerParams(
            collective_id=0, has_side_effects=True, vmem_limit_bytes=VMEM_LIMIT
        ),
        name="relay_attention",
    )(order, image_index, lengths, picks, queries, cross_query_rows, image_cache, gate)
    attended = jnp.take(by_rank, length_rank, axis=0)
    attended = attended.reshape(requests, KEY_HEAD_COUNT, QUERY_PER_KEY, local, HEAD_WIDTH)
    attended = jnp.transpose(attended, (3, 0, 1, 2, 4)).reshape(local, requests, HQ * HEAD_WIDTH)

    length = jnp.sum(jnp.where(owner_slot == rank, lengths, 0))
    own = owned.reshape(slot, width)
    own = jnp.where(jnp.arange(slot, dtype=jnp.int32)[:, None] < length, own, jnp.zeros((), own.dtype))
    kv_cache = jnp.stack([own[:, : width // 2], own[:, width // 2 :]])[:, None]
    return attended, kv_cache


def solution(mesh):
    placed = (
        P("tok", "groups", None),
        P("tok", "groups", None),
        P("tok", "groups", None),
        P("tok", "groups", None),
        P(None, "groups", None, None),
        P(),
        P("groups"),
        P("groups"),
        P("groups"),
    )
    return jax.shard_map(
        relayed if mesh.shape["tok"] == 16 else shards,
        mesh=mesh,
        in_specs=placed,
        out_specs=(P("tok", "groups", None), P(None, ("groups", "tok"), None, None)),
        check_vma=False,
    )
```

```python
import functools
import math

import jax
import jax.numpy as jnp
from jax import lax
from jax.experimental import pallas as pl
from jax.experimental.pallas import tpu as pltpu
from jax.sharding import PartitionSpec as P

HQ = 32
KEY_HEAD_COUNT = 4
HEAD_WIDTH = 128
QUERY_PER_KEY = 8
SCALE = 1.0 / math.sqrt(HEAD_WIDTH)
VMEM_LIMIT = 52 * 1024 * 1024

NT = (((1,), (1,)), ((), ()))


def attend(queries, keys, values, bias):
    scores = lax.dot_general(queries, keys, NT, preferred_element_type=jnp.float32) * SCALE
    if bias is not None:
        scores = scores + bias
    top = jnp.max(scores, axis=-1, keepdims=True)
    weights = jnp.exp(scores - top)
    total = jnp.sum(weights, axis=-1, keepdims=True)
    weighted = jnp.dot(weights.astype(jnp.bfloat16), values, preferred_element_type=jnp.float32)
    return weighted, total


def cross_kernel(local, lengths_ref, image_ref, first_ref, query_ref, cache_ref, gate_ref, out_ref):
    request = pl.program_id(0)
    live = lengths_ref[request] > first_ref[0]

    @pl.when(live)
    def _():
        picture = image_ref[request]
        for group in range(KEY_HEAD_COUNT):
            lanes = slice(group * HEAD_WIDTH, (group + 1) * HEAD_WIDTH)
            weighted, total = attend(
                query_ref[0, group], cache_ref[0, picture, :, lanes], cache_ref[1, picture, :, lanes], None
            )
            out_ref[0, group] = (weighted * (gate_ref[group] / total)).astype(out_ref.dtype)

    @pl.when(jnp.logical_not(live))
    def _():
        out_ref[...] = jnp.zeros_like(out_ref)


def causal_kernel(local, slot, lengths_ref, first_ref, query_ref, kv_ref, cross_ref, out_ref):
    request = pl.program_id(0)
    first = first_ref[0]
    length = lengths_ref[request]
    live = length > first
    rows = QUERY_PER_KEY * local
    needed = first + local

    def run(keys):
        row = lax.broadcasted_iota(jnp.int32, (rows, keys), 0)
        position = first + lax.rem(row, local)
        key = lax.broadcasted_iota(jnp.int32, (rows, keys), 1)
        bias = jnp.where(key <= position, 0.0, -1e30)
        alive = position[:, :HEAD_WIDTH] < length
        for group in range(KEY_HEAD_COUNT):
            lanes = slice(group * HEAD_WIDTH, (group + 1) * HEAD_WIDTH)
            value_lanes = slice((KEY_HEAD_COUNT + group) * HEAD_WIDTH, (KEY_HEAD_COUNT + group + 1) * HEAD_WIDTH)
            weighted, total = attend(
                query_ref[0, group], kv_ref[0, :keys, lanes], kv_ref[0, :keys, value_lanes], bias
            )
            own = (weighted / total).astype(jnp.bfloat16).astype(jnp.float32)
            combined = own + cross_ref[0, group].astype(jnp.float32)
            out_ref[0, group] = jnp.where(alive, combined, 0.0).astype(out_ref.dtype)

    for keys in range(128, slot + 1, 128):
        @pl.when(live & (needed <= keys) & (needed > keys - 128))
        def _():
            run(keys)

    @pl.when(jnp.logical_not(live))
    def _():
        out_ref[...] = jnp.zeros_like(out_ref)


def shards(
    queries,
    cross_query_rows,
    prompt_key_rows,
    prompt_value_rows,
    image_cache,
    query_head_gate,
    lengths,
    owner_slot,
    image_index,
):
    local, requests, _ = queries.shape
    devices = lax.axis_size("tok")
    slot = local * devices
    rank = lax.axis_index("tok")
    rows = QUERY_PER_KEY * local
    first = jnp.full((1,), rank * local, jnp.int32)

    kv = jnp.concatenate([prompt_key_rows, prompt_value_rows], axis=-1)
    gathered = lax.all_gather(kv, "tok", axis=0, tiled=True)
    by_request = jnp.transpose(gathered, (1, 0, 2))

    def by_head(array):
        array = array.reshape(local, requests, KEY_HEAD_COUNT, QUERY_PER_KEY, HEAD_WIDTH)
        return jnp.transpose(array, (1, 2, 3, 0, 4)).reshape(requests, KEY_HEAD_COUNT, rows, HEAD_WIDTH)

    gate = jnp.tanh(query_head_gate).reshape(KEY_HEAD_COUNT, QUERY_PER_KEY, 1)
    gate = jnp.broadcast_to(gate, (KEY_HEAD_COUNT, QUERY_PER_KEY, local)).reshape(KEY_HEAD_COUNT, rows, 1)

    head_block = pl.BlockSpec((1, KEY_HEAD_COUNT, rows, HEAD_WIDTH), lambda r, *_: (r, 0, 0, 0))
    head_shape = jax.ShapeDtypeStruct((requests, KEY_HEAD_COUNT, rows, HEAD_WIDTH), jnp.bfloat16)
    params = pltpu.CompilerParams(vmem_limit_bytes=VMEM_LIMIT)
    flops = requests * HQ * local * HEAD_WIDTH * 4
    cross = pl.pallas_call(
        functools.partial(cross_kernel, local),
        grid_spec=pltpu.PrefetchScalarGridSpec(
            num_scalar_prefetch=3,
            grid=(requests,),
            in_specs=[
                head_block,
                pl.BlockSpec(image_cache.shape, lambda r, *_: (0, 0, 0, 0)),
                pl.BlockSpec(gate.shape, lambda r, *_: (0, 0, 0)),
            ],
            out_specs=head_block,
        ),
        out_shape=head_shape,
        compiler_params=params,
        cost_estimate=pl.CostEstimate(flops=flops * 512, bytes_accessed=8 << 20, transcendentals=0),
        name="cross",
    )(lengths, image_index, first, by_head(cross_query_rows), image_cache, gate)

    attended = pl.pallas_call(
        functools.partial(causal_kernel, local, slot),
        grid_spec=pltpu.PrefetchScalarGridSpec(
            num_scalar_prefetch=2,
            grid=(requests,),
            in_specs=[
                head_block,
                pl.BlockSpec((1, slot, 2 * KEY_HEAD_COUNT * HEAD_WIDTH), lambda r, *_: (r, 0, 0)),
                head_block,
            ],
            out_specs=head_block,
        ),
        out_shape=head_shape,
        compiler_params=params,
        cost_estimate=pl.CostEstimate(flops=flops * slot, bytes_accessed=24 << 20, transcendentals=0),
        name="causal",
    )(lengths, first, by_head(queries), by_request, cross)
    attended = attended.reshape(requests, KEY_HEAD_COUNT, QUERY_PER_KEY, local, HEAD_WIDTH)
    attended = jnp.transpose(attended, (3, 0, 1, 2, 4)).reshape(local, requests, HQ * HEAD_WIDTH)

    own_request = jnp.argmax(owner_slot == rank).astype(jnp.int32)
    length = lax.dynamic_index_in_dim(lengths, own_request, 0, keepdims=False)
    own = lax.dynamic_index_in_dim(by_request, own_request, 0, keepdims=False)
    own = jnp.where(jnp.arange(slot, dtype=jnp.int32)[:, None] < length, own, jnp.zeros((), own.dtype))
    width = KEY_HEAD_COUNT * HEAD_WIDTH
    kv_cache = jnp.stack([own[:, :width], own[:, width:]])[:, None]
    return attended, kv_cache


CHUNK = 8
STEP_US = 1.5
TURN_STEPS = 8
LINK_BYTES_PER_US = 45000.0
SCALE_LOG2 = SCALE * math.log2(math.e)


def rank_limit(requests, slot, first):
    if first == 0:
        return requests
    return min(requests, (requests * slot // 2 - requests) // first)


def relay_plan(chips, requests, slot, local):
    span = slot // chips
    limit = [rank_limit(requests, slot, span * chip) for chip in range(chips)]
    chunks = [(0, CHUNK), (CHUNK, requests)]

    def ranks(chip, chunk, up):
        lo, hi = chunks[chunk]
        top = limit[chip - chip % 2] if up else limit[chip]
        return lo, max(lo, min(hi, top))

    free = {}
    rate = local * 2048 / LINK_BYTES_PER_US
    pending = []
    for chip in range(chips):
        pending.append((0.0, chip, chip, "own", 0))
        pending.append((rate * CHUNK * (chip // 2 + 1), chip, chip, "own", 1))
    events = [[] for _ in range(chips)]
    while pending:
        pending.sort()
        time, chip, source, via, chunk = pending.pop(0)
        sends = []
        if via != "side":
            if chip + 2 < chips:
                sends.append((chip + 2, "up"))
            if source < (chip ^ 1):
                sends.append((chip ^ 1, "side"))
        kept = []
        for target, way in sends:
            lo, hi = ranks(target, chunk, way == "up")
            if hi > lo:
                start = max(time, free.get((chip, target), 0.0))
                end = start + rate * (hi - lo)
                free[chip, target] = end
                pending.append((end + 1.0, target, source, way, chunk))
                kept.append((target, lo, hi))
        got = ranks(chip, chunk, via == "up")
        need = ranks(chip, chunk, False)
        events[chip].append((time, source, via, chunk, got, need, kept))

    cross_steps, causal_steps = [], []
    for chip in range(chips):
        last = max(position for position, event in enumerate(events[chip]) if event[3] == 0)
        early, late = {}, {}
        base = max(limit[chip], int(events[chip][last][0] / STEP_US) + 1)
        for position, event in enumerate(events[chip]):
            step = int(event[0] / STEP_US)
            if step < limit[chip]:
                early.setdefault(step, []).append(position)
            elif position <= last:
                late.setdefault(0, []).append(position)
            else:
                late.setdefault(max(0, min(CHUNK, step - base)), []).append(position)
        cross_steps.append(early)
        causal_steps.append(late)
    return limit, events, cross_steps, causal_steps


def weigh(scores, values):
    top = jnp.max(scores, axis=-1, keepdims=True)
    weights = jnp.exp2((scores - top) * SCALE_LOG2)
    total = jnp.sum(weights, axis=-1, keepdims=True)
    return jnp.dot(weights.astype(jnp.bfloat16), values, preferred_element_type=jnp.float32), total


def relay_kernel(
    devices, requests, local, slot, plan,
    order_ref, image_ref, lengths_ref, picks_ref, query_ref, cross_query_ref, cache_ref, gate_ref,
    out_ref, owned_ref, kv_ref, turned_ref, turned_cross_ref, send_sem, recv_sem, pass_sem, owned_send, owned_recv, local_sem,
):
    limit, events, cross_steps, causal_steps = plan
    me = lax.axis_index("tok")
    chip, core = lax.div(me, 2), lax.rem(me, 2)
    rows = QUERY_PER_KEY * local
    first = me * local
    needed = first + local
    barrier = pltpu.get_barrier_semaphore()

    def greet(offset, carry):
        pl.semaphore_signal(
            barrier, inc=1, device_id={"tok": lax.rem(me + offset, devices)}, device_id_type=pl.DeviceIdType.MESH
        )
        return carry

    lax.fori_loop(1, devices, greet, 0)
    pl.semaphore_wait(barrier, devices - 1)

    keep = pltpu.make_async_copy(picks_ref.at[pl.ds(0, requests)], kv_ref.at[me], local_sem.at[0])
    keep_owned = pltpu.make_async_copy(picks_ref.at[requests + me], owned_ref.at[me], local_sem.at[1])

    def relay(source, lo, hi, chunk, target, send, own):
        here = picks_ref.at[pl.ds(lo, hi - lo)] if own else kv_ref.at[source, pl.ds(lo, hi - lo)]
        return pltpu.make_async_remote_copy(
            src_ref=here,
            dst_ref=kv_ref.at[source, pl.ds(lo, hi - lo)],
            send_sem=send,
            recv_sem=recv_sem.at[2 * source + chunk],
            device_id={"tok": target},
            device_id_type=pl.DeviceIdType.MESH,
        )

    def copies(number, position):
        _, source_chip, via, chunk, _, need, sends = events[number][position]
        source = 2 * source_chip + core
        result = []
        for index, (target, lo, hi) in enumerate(sends):
            result.append(
                relay(source, lo, hi, chunk, 2 * target + core, send_sem.at[index, 2 * source_chip + chunk], via == "own")
            )
        if need[1] > need[0]:
            result.append(
                relay(source, need[0], need[1], chunk, 2 * number + 1 - core, pass_sem.at[2 * source_chip + chunk], via == "own")
            )
        return result

    def handle(number, position):
        _, source_chip, via, chunk, got, _, _ = events[number][position]
        if via != "own":
            relay(2 * source_chip + core, got[0], got[1], chunk, me, pass_sem.at[0], False).wait_recv()
        for copy in copies(number, position):
            copy.start()

    def wait_passed(number, wanted):
        for _, source_chip, _, chunk, _, need, _ in events[number]:
            if chunk == wanted and need[1] > need[0]:
                relay(2 * source_chip + 1 - core, need[0], need[1], chunk, me, pass_sem.at[0], False).wait_recv()

    def owned_copy(offset):
        target = lax.rem(me + offset, devices)
        return pltpu.make_async_remote_copy(
            src_ref=picks_ref.at[requests + target],
            dst_ref=owned_ref.at[me],
            send_sem=owned_send.at[offset],
            recv_sem=owned_recv.at[offset],
            device_id={"tok": target},
            device_id_type=pl.DeviceIdType.MESH,
        )

    def owned_start(offset, carry):
        owned_copy(offset).start()
        return carry

    count = limit[0]
    for number in range(1, devices // 2):
        count = jnp.where(chip == number, limit[number], count)

    def events_at(steps, step, last):
        for number in range(devices // 2):
            @pl.when(chip == number)
            def _():
                for when in sorted(set(steps[number]) | set(last)):
                    @pl.when(step == when)
                    def _():
                        for position in steps[number].get(when, ()):
                            handle(number, position)
                        if when in last:
                            wait_passed(number, last[when])

    def turn(source_ref, target_ref, head):
        lanes = pl.ds(pl.multiple_of(head * HEAD_WIDTH, HEAD_WIDTH), HEAD_WIDTH)
        target_ref[:, head] = jnp.swapaxes(source_ref[:, :, lanes].astype(jnp.float32), 0, 1)

    def turn_cross(head, carry):
        turn(cross_query_ref, turned_cross_ref, head)
        return carry

    def turn_own(head, carry):
        turn(query_ref, turned_ref, head)
        return carry

    def head_rows(turned, request, group):
        part = turned[request, group * QUERY_PER_KEY : (group + 1) * QUERY_PER_KEY]
        return part.reshape(rows, HEAD_WIDTH).astype(jnp.bfloat16)

    def cross_step(place, carry):
        events_at(cross_steps, place, {})

        @pl.when(place == 0)
        def _():
            keep.start()
            keep_owned.start()
            lax.fori_loop(devices - me, devices, owned_start, 0)
            lax.fori_loop(0, HQ, turn_cross, 0)

        @pl.when(place < TURN_STEPS)
        def _():
            lax.fori_loop(place * (HQ // TURN_STEPS), (place + 1) * (HQ // TURN_STEPS), turn_own, 0)

        request = order_ref[place]
        picture = image_ref[request]
        for group in range(KEY_HEAD_COUNT):
            lanes = slice(group * HEAD_WIDTH, (group + 1) * HEAD_WIDTH)
            scores = lax.dot_general(
                head_rows(turned_cross_ref, request, group), cache_ref[0, picture, :, lanes], NT, preferred_element_type=jnp.float32
            )
            weighted, total = weigh(scores, cache_ref[1, picture, :, lanes])
            out_ref[place, group] = (weighted * (gate_ref[group] / total)).astype(out_ref.dtype)
        return carry

    lax.fori_loop(0, count, cross_step, 0)
    keep.wait()

    def run(place, keys):
        request = order_ref[place]
        sources = -(-keys // local)
        row = lax.broadcasted_iota(jnp.int32, (rows, keys), 0)
        position = first + lax.rem(row, local)
        key = lax.broadcasted_iota(jnp.int32, (rows, keys), 1)
        allowed = key <= position
        alive = position[:, :HEAD_WIDTH] < lengths_ref[request]
        written = lax.broadcasted_iota(jnp.int32, (keys, HEAD_WIDTH), 0) < needed

        def rows_of(lane_block):
            lanes = slice(lane_block * HEAD_WIDTH, (lane_block + 1) * HEAD_WIDTH)
            pieces = kv_ref[:sources, place, :, lanes].astype(jnp.float32)
            return pieces.reshape(sources * local, HEAD_WIDTH)[:keys]

        for group in range(KEY_HEAD_COUNT):
            key_rows = rows_of(group).astype(jnp.bfloat16)
            value_rows = jnp.where(written, rows_of(KEY_HEAD_COUNT + group), 0.0).astype(jnp.bfloat16)
            scores = lax.dot_general(
                head_rows(turned_ref, request, group), key_rows, NT, preferred_element_type=jnp.float32
            )
            weighted, total = weigh(jnp.where(allowed, scores, -1e30), value_rows)
            own = (weighted / total).astype(jnp.bfloat16).astype(jnp.float32)
            combined = own + out_ref[place, group].astype(jnp.float32)
            out_ref[place, group] = jnp.where(alive, combined, 0.0).astype(out_ref.dtype)

    def causal_step(place, carry):
        events_at(causal_steps, place, {0: 0, CHUNK: 1})

        @pl.when(place == 0)
        def _():
            lax.fori_loop(1, devices - me, owned_start, 0)

        for keys in range(128, slot + 1, 128):
            @pl.when((needed <= keys) & (needed > keys - 128))
            def _():
                run(place, keys)

        return carry

    lax.fori_loop(0, count, causal_step, 0)

    def clear(place, carry):
        out_ref[place] = jnp.zeros(out_ref.shape[1:], out_ref.dtype)
        return carry

    lax.fori_loop(count, requests, clear, 0)

    for number in range(devices // 2):
        @pl.when(chip == number)
        def _():
            for position in range(len(events[number])):
                for copy in copies(number, position):
                    copy.wait_send()

    def owned_wait(offset, carry):
        source = lax.rem(me + devices - offset, devices)
        pltpu.make_async_remote_copy(
            src_ref=picks_ref.at[requests + me],
            dst_ref=owned_ref.at[source],
            send_sem=owned_send.at[offset],
            recv_sem=owned_recv.at[offset],
            device_id={"tok": source},
            device_id_type=pl.DeviceIdType.MESH,
        ).wait_recv()
        owned_copy(offset).wait_send()
        return carry

    lax.fori_loop(1, devices, owned_wait, 0)
    keep_owned.wait()


def relayed(
    queries,
    cross_query_rows,
    prompt_key_rows,
    prompt_value_rows,
    image_cache,
    query_head_gate,
    lengths,
    owner_slot,
    image_index,
):
    local, requests, _ = queries.shape
    devices = lax.axis_size("tok")
    slot = local * devices
    rank = lax.axis_index("tok")
    rows = QUERY_PER_KEY * local
    width = 2 * KEY_HEAD_COUNT * HEAD_WIDTH
    first = jnp.full((1,), rank * local, jnp.int32)
    ids = jnp.arange(requests, dtype=jnp.int32)

    longer = lengths[None, :] > lengths[:, None]
    tied = (lengths[None, :] == lengths[:, None]) & (ids[None, :] < ids[:, None])
    length_rank = jnp.sum((longer | tied).astype(jnp.int32), axis=1)
    chosen = jnp.concatenate([length_rank, owner_slot + requests]).reshape(2, requests)
    places = jnp.arange(2 * requests, dtype=jnp.int32)
    pick = (places[:, None, None] == chosen[None]).any(axis=1).astype(jnp.bfloat16)
    kv = jnp.concatenate([prompt_key_rows, prompt_value_rows], axis=-1)
    picks = jnp.einsum("sr,lrd->sld", pick, kv, preferred_element_type=jnp.float32).astype(jnp.bfloat16)

    gate = jnp.tanh(query_head_gate).reshape(KEY_HEAD_COUNT, QUERY_PER_KEY, 1)
    gate = jnp.broadcast_to(gate, (KEY_HEAD_COUNT, QUERY_PER_KEY, local)).reshape(KEY_HEAD_COUNT, rows, 1)

    head_shape = jax.ShapeDtypeStruct((requests, KEY_HEAD_COUNT, rows, HEAD_WIDTH), jnp.bfloat16)
    anywhere = pl.BlockSpec(memory_space=pl.ANY)
    vmem = pl.BlockSpec(memory_space=pltpu.VMEM)
    plan = relay_plan(devices // 2, requests, slot, local)
    order = jnp.sum(ids[:, None] * (length_rank[:, None] == ids[None, :]), axis=0).astype(jnp.int32)
    smem = pl.BlockSpec(memory_space=pltpu.SMEM)
    by_rank, owned = pl.pallas_call(
        functools.partial(relay_kernel, devices, requests, local, slot, plan),
        in_specs=[smem, smem, smem, vmem, vmem, vmem, vmem, vmem],
        out_specs=[vmem, anywhere],
        out_shape=[head_shape, jax.ShapeDtypeStruct((devices, local, width), jnp.bfloat16)],
        scratch_shapes=[
            pltpu.VMEM((devices, requests, local, width), jnp.bfloat16),
            pltpu.VMEM((requests, HQ, local, HEAD_WIDTH), jnp.float32),
            pltpu.VMEM((requests, HQ, local, HEAD_WIDTH), jnp.float32),
            pltpu.SemaphoreType.DMA((2, devices)),
            pltpu.SemaphoreType.DMA((2 * devices,)),
            pltpu.SemaphoreType.DMA((devices,)),
            pltpu.SemaphoreType.DMA((devices,)),
            pltpu.SemaphoreType.DMA((devices,)),
            pltpu.SemaphoreType.DMA((2,)),
        ],
        compiler_params=pltpu.CompilerParams(
            collective_id=0, has_side_effects=True, vmem_limit_bytes=VMEM_LIMIT
        ),
        name="relay_attention",
    )(order, image_index, lengths, picks, queries, cross_query_rows, image_cache, gate)
    attended = jnp.take(by_rank, length_rank, axis=0)
    attended = attended.reshape(requests, KEY_HEAD_COUNT, QUERY_PER_KEY, local, HEAD_WIDTH)
    attended = jnp.transpose(attended, (3, 0, 1, 2, 4)).reshape(local, requests, HQ * HEAD_WIDTH)

    length = jnp.sum(jnp.where(owner_slot == rank, lengths, 0))
    own = owned.reshape(slot, width)
    own = jnp.where(jnp.arange(slot, dtype=jnp.int32)[:, None] < length, own, jnp.zeros((), own.dtype))
    kv_cache = jnp.stack([own[:, : width // 2], own[:, width // 2 :]])[:, None]
    return attended, kv_cache


def solution(mesh):
    placed = (
        P("tok", "groups", None),
        P("tok", "groups", None),
        P("tok", "groups", None),
        P("tok", "groups", None),
        P(None, "groups", None, None),
        P(),
        P("groups"),
        P("groups"),
        P("groups"),
    )
    return jax.shard_map(
        relayed if mesh.shape["tok"] == 16 else shards,
        mesh=mesh,
        in_specs=placed,
        out_specs=(P("tok", "groups", None), P(None, ("groups", "tok"), None, None)),
        check_vma=False,
    )
```
